32 devices in a mesh: seq: 8 (over z, y), batch: 4 (over x, core).
Axes of the slice: x: 2, y: 2, z: 4, core: 2. Of those that a mesh axis runs over, the one named last changes fastest.
Arguments:
- tokens: bfloat16 [16, 2048, 1024], P('batch', 'seq'), may hold values from -6 to 6
- cotangent: bfloat16 [16, 2048, 1024], P('batch', 'seq'), may hold values from -6 to 6
- log_decay: float32 [16, 2048], P(None, 'seq'), may hold values from -2.6 to 0
- w_mix: float32 [4, 1024, 1024], P(None, 'batch'), may hold values from -0.1875 to 0.1875
- w_out: float32 [1024, 1024], P('batch'), may hold values from -0.25 to 0.25
- w_in: float32 [2, 2816, 1024], P(None, 'batch'), may hold values from -0.1875 to 0.1875
- w_down: float32 [2816, 1024], P('batch'), may hold values from -0.109375 to 0.109375
- m_mix: float32 [4, 1024, 1024], P(None, 'batch'), may hold values from -512 to 512
- m_out: float32 [1024, 1024], P('batch'), may hold values from -512 to 512
- m_in: float32 [2, 2816, 1024], P(None, 'batch'), may hold values from -512 to 512
- m_down: float32 [2816, 1024], P('batch'), may hold values from -512 to 512
Outputs:
- activations: bfloat16 [16, 2048, 1024], P('batch', 'seq')
- input_grad: bfloat16 [16, 2048, 1024], P('batch', 'seq')
- mom_mix: float32 [4, 1024, 1024], P(None, 'batch')
- mom_out: float32 [1024, 1024], P('batch')
- mom_in: float32 [2, 2816, 1024], P(None, 'batch')
- mom_down: float32 [2816, 1024], P('batch')
- new_mix: float32 [4, 1024, 1024], P(None, 'batch')
- new_out: float32 [1024, 1024], P('batch')
- new_in: float32 [2, 2816, 1024], P(None, 'batch')
- new_down: float32 [2816, 1024], P('batch')
- copy_mix: bfloat16 [4, 1024, 1024], P(None, 'batch')
- copy_out: bfloat16 [1024, 1024], P('batch')
- copy_in: bfloat16 [2, 2816, 1024], P(None, 'batch')
- copy_down: bfloat16 [2816, 1024], P('batch')
The draws below stay inside these ranges and needn't reach their ends.
All inputs are finite; a program needn't handle non-finite values.
Results may differ from the reference program's by a relative error of at most 0.03.
Values may be sent and summed in bfloat16 or wider, within the bound.
No kernel may reach another device: no remote copies, remote signals or barrier semaphores. Data moves between devices by JAX's collectives and lax.ppermute only.
A program may use at most 384 MiB of HBM per device.

```python
import jax
import jax.numpy as jnp
from jax import lax

D = 1024
HEAD_COUNT = 16
HEAD_DIM = 64
FF = 2816
SEQUENCE_LENGTH = 2048
ITERS = 5
GROUP = 256
NSEQ = 16


def draw_log_decay(key, part):
    key = jax.random.fold_in(key, 11)
    random_keys = jax.random.split(key, 7)
    fast_share = 0.5
    fast_heads = jax.random.uniform(random_keys[0], (HEAD_COUNT, 1)) < fast_share
    slow_rate = jax.random.uniform(random_keys[1], (HEAD_COUNT, 1), minval=0.1, maxval=1.0) * 0.6 / SEQUENCE_LENGTH
    fast_rate = jax.random.uniform(random_keys[2], (HEAD_COUNT, 1), minval=0.06, maxval=0.12)
    baseline_rate = jnp.where(fast_heads, fast_rate, slow_rate)
    machine_factor = jnp.exp(jax.random.uniform(random_keys[3], (HEAD_COUNT, SEQUENCE_LENGTH // GROUP), minval=-0.69, maxval=0.69))
    machine_factor = jnp.repeat(machine_factor, GROUP, axis=1)
    coarse_factor = jnp.exp(jax.random.uniform(random_keys[4], (HEAD_COUNT, SEQUENCE_LENGTH), minval=-0.69, maxval=0.69))
    spike_locations = jax.random.randint(random_keys[5], (HEAD_COUNT, 3), 0, SEQUENCE_LENGTH)
    spike_depth = jax.random.uniform(random_keys[6], (HEAD_COUNT, 3), minval=0.22, maxval=0.69)
    token_positions = jnp.arange(SEQUENCE_LENGTH)
    spike_loss = jnp.sum(jnp.where(spike_locations[:, :, None] == token_positions[None, None, :], spike_depth[:, :, None], 0.0), axis=1)
    return -(baseline_rate * machine_factor * coarse_factor + spike_loss)


def block_scale(key, extent, cuts, least, high):
    level = 1.0
    for axis_at, blocks in cuts:
        steps = jax.random.uniform(jax.random.fold_in(jax.random.fold_in(key, 6), axis_at), (blocks,), jnp.float32, least / len(cuts), high / len(cuts))
        level = level * jnp.repeat(jnp.exp(steps), extent[axis_at] // blocks).reshape((-1,) + (1,) * (len(extent) - 1 - axis_at))
    return level


def bell_draw(rng, extent, scale, limit, cuts=(), kind=jnp.bfloat16):
    factor_of = block_scale(rng, extent, cuts, -0.22, 0.18) if cuts else 1.0
    drawn = jax.random.normal(rng, extent, jnp.float32) * scale * factor_of
    return jnp.minimum(jnp.maximum(drawn, -limit), limit).astype(kind)


def setup_inputs(seed: int = 0) -> dict:
    keys = jax.random.split(jax.random.key(seed), 12)
    return {
        "tokens": bell_draw(keys[0], (NSEQ, SEQUENCE_LENGTH, D), 1.0, 6.0, ((0, 4), (1, 8))),
        "cotangent": bell_draw(keys[1], (NSEQ, SEQUENCE_LENGTH, D), 1.0, 6.0, ((0, 4), (1, 8))),
        "log_decay": draw_log_decay(jax.random.fold_in(keys[11], 71), 0),
        "w_mix": bell_draw(keys[3], (4, D, D), D ** -0.5, 0.1875, ((1, 4),), jnp.float32),
        "w_out": bell_draw(keys[4], (D, D), (D // 2) ** -0.5, 0.25, ((0, 4),), jnp.float32),
        "w_in": bell_draw(keys[5], (2, FF, D), D ** -0.5, 0.1875, ((1, 4),), jnp.float32),
        "w_down": bell_draw(keys[6], (FF, D), FF ** -0.5, 0.109375, ((0, 4),), jnp.float32),
        "m_mix": bell_draw(keys[7], (4, D, D), (0.5 * (NSEQ * SEQUENCE_LENGTH) ** 0.5), 512.0, ((1, 4),), jnp.float32),
        "m_out": bell_draw(keys[8], (D, D), (0.5 * (NSEQ * SEQUENCE_LENGTH) ** 0.5), 512.0, ((0, 4),), jnp.float32),
        "m_in": bell_draw(keys[9], (2, FF, D), (0.5 * (NSEQ * SEQUENCE_LENGTH) ** 0.5), 512.0, ((1, 4),), jnp.float32),
        "m_down": bell_draw(keys[10], (FF, D), (0.5 * (NSEQ * SEQUENCE_LENGTH) ** 0.5), 512.0, ((0, 4),), jnp.float32),
    }


EPSILON = 1e-06
NORM_FLOOR = 1e-07
COEFF_A = 3.4445
COEFF_B = -4.775
COEFF_C = 2.0315
MOMENTUM = 0.5
STEP_RATE = 0.8
PRECISE = lax.Precision.HIGHEST

@jax.custom_vjp
def low(v):
    return lax.optimization_barrier(v.astype(jnp.bfloat16)).astype(jnp.float32)

@jax.custom_vjp
def low_back(v):
    return v

def low_keep(v):
    return (low(v), None)

def low_pass(kept, grad):
    return (grad,)

def back_keep(v):
    return (v, None)

def back_low(kept, grad):
    return (low(grad),)
low.defvjp(low_keep, low_pass)
low_back.defvjp(back_keep, back_low)

def normalize(inputs):
    return inputs * lax.rsqrt(lax.optimization_barrier(jnp.mean(inputs * inputs, axis=-1, keepdims=True)) + EPSILON)

def mat_mul(left, right):
    return jnp.dot(left, right, precision=PRECISE)

def attend(queries, keys_act, values_in, log_decay):
    group_count = SEQUENCE_LENGTH // GROUP

    def split_heads(array_in):
        return array_in.reshape(group_count, GROUP, HEAD_COUNT, HEAD_DIM)
    decay_blocks = log_decay.reshape(HEAD_COUNT, group_count, GROUP).transpose(1, 0, 2)
    causal = lax.broadcasted_iota(jnp.int32, (GROUP, GROUP), 0) >= lax.broadcasted_iota(jnp.int32, (GROUP, GROUP), 1)

    def group_step(carry_state, pieces):
        q_blk, k_blk, v_blk, ld_blk = pieces
        cum_decay = jnp.cumsum(ld_blk, axis=1)
        last_cum = cum_decay[:, -1]
        spread = cum_decay[:, :, None] - cum_decay[:, None, :]
        decay_mask = jnp.where(causal[None], jnp.exp(jnp.where(causal[None], spread, 0.0)), 0.0)
        scores = jnp.einsum('the,she->hts', q_blk, k_blk, precision=PRECISE) * decay_mask
        result = jnp.einsum('hts,shf->thf', scores, v_blk, precision=PRECISE)
        result = result + jnp.einsum('the,ht,hef->thf', q_blk, jnp.exp(cum_decay), carry_state, precision=PRECISE)
        trail_decay = jnp.exp(last_cum[:, None] - cum_decay)
        summary = jnp.einsum('she,hs,shf->hef', k_blk, trail_decay, v_blk, precision=PRECISE)
        return (jnp.exp(last_cum)[:, None, None] * carry_state + summary, result)
    zero_state = jnp.zeros((HEAD_COUNT, HEAD_DIM, HEAD_DIM), jnp.float32)
    _, results = lax.scan(jax.checkpoint(group_step), zero_state, (split_heads(queries), split_heads(keys_act), split_heads(values_in), decay_blocks))
    return results.reshape(SEQUENCE_LENGTH, HEAD_COUNT * HEAD_DIM)

def block_layer(sequence, mix_w, out_w, in_w, down_w, log_decay):
    normed = low(normalize(sequence))
    projected = [low_back(mat_mul(normed, mix_w[member])) for member in range(4)]
    queries = jax.nn.silu(projected[0])
    keys_act = jax.nn.silu(projected[1])
    gate_act = jax.nn.silu(projected[3])
    attended = attend(queries, keys_act, projected[2], log_decay)
    hidden = low(normalize(attended) * gate_act)
    middle = low_back(sequence + mat_mul(hidden, out_w))
    normed_ffn = low(normalize(middle))
    first_term = low_back(mat_mul(normed_ffn, in_w[0].T))
    second = low_back(mat_mul(normed_ffn, in_w[1].T))
    product = low(first_term * second)
    return middle + mat_mul(product, down_w)

def newton(momentum):
    rough_mat = lax.optimization_barrier(momentum.astype(jnp.bfloat16)).astype(jnp.float32)
    norm_size = jnp.sqrt(jnp.sum(rough_mat * rough_mat)) + NORM_FLOOR
    iterate = (rough_mat / norm_size).astype(jnp.bfloat16)
    for number in range(ITERS):
        gram = jnp.dot(iterate.T, iterate, preferred_element_type=jnp.float32).astype(jnp.bfloat16)
        first_term = jnp.dot(iterate, gram, preferred_element_type=jnp.float32)
        second = jnp.dot(first_term.astype(jnp.bfloat16), gram, preferred_element_type=jnp.float32)
        iterate = (COEFF_A * iterate.astype(jnp.float32) + COEFF_B * first_term + COEFF_C * second).astype(jnp.bfloat16)
    return iterate

def update(weight, momentum, factor):
    return weight - STEP_RATE * factor * newton(momentum).astype(jnp.float32)

def reference(tokens, cotangent, log_decay, w_mix, w_out, w_in, w_down, m_mix, m_out, m_in, m_down):

    def as_used(weight):
        return lax.optimization_barrier(weight.astype(jnp.bfloat16)).astype(jnp.float32)

    def forward(inputs, mix_w, out_w, in_w, down_w):

        def per_sequence(sequence):
            return jax.checkpoint(block_layer)(sequence, mix_w, out_w, in_w, down_w, log_decay)
        return lax.map(per_sequence, inputs)
    output, pull_back = jax.vjp(forward, tokens.astype(jnp.float32), as_used(w_mix), as_used(w_out), as_used(w_in), as_used(w_down))
    grads = pull_back(cotangent.astype(jnp.float32))
    mom_mix = MOMENTUM * m_mix + grads[1]
    mom_out = MOMENTUM * m_out + grads[2]
    mom_in = MOMENTUM * m_in + grads[3]
    mom_down = MOMENTUM * m_down + grads[4]
    wide_factor = (FF / D) ** 0.5
    new_mix = jnp.stack([update(w_mix[member], mom_mix[member], 1.0) for member in range(4)])
    new_out = update(w_out, mom_out, 1.0)
    new_in = jnp.stack([update(w_in[member], mom_in[member], wide_factor) for member in range(2)])
    new_down = update(w_down, mom_down, 1.0)
    return (output.astype(jnp.bfloat16), grads[0].astype(jnp.bfloat16), mom_mix, mom_out, mom_in, mom_down, new_mix, new_out, new_in, new_down, new_mix.astype(jnp.bfloat16), new_out.astype(jnp.bfloat16), new_in.astype(jnp.bfloat16), new_down.astype(jnp.bfloat16))
```

```python
import math

import jax
import jax.numpy as jnp
from jax import lax
from jax.experimental import pallas as pl
from jax.experimental.pallas import tpu as pltpu
from jax.sharding import PartitionSpec as P

D = 1024
HEAD_COUNT = 16
HEAD_DIM = 64
FF = 2816
ITERS = 5
PAIRS = HEAD_COUNT // 2
LANES = 2 * HEAD_DIM
TILE = 256
HEADS_PER_TILE = TILE // HEAD_DIM
PAIRS_PER_TILE = TILE // LANES
QUADS = 4

EPSILON = 1e-06
NORM_FLOOR = 1e-07
COEFF_A = 3.4445
COEFF_B = -4.775
COEFF_C = 2.0315
MOMENTUM = 0.5
STEP_RATE = 0.8

F32 = jnp.float32
BF16 = jnp.bfloat16
MIB = 1024 * 1024


def dot_nn(left, right):
    return lax.dot_general(left, right, (((1,), (0,)), ((), ())), preferred_element_type=F32)


def dot_nt(left, right):
    return lax.dot_general(left, right, (((1,), (1,)), ((), ())), preferred_element_type=F32)


def dot_tn(left, right):
    return lax.dot_general(left, right, (((0,), (0,)), ((), ())), preferred_element_type=F32)


def silu_grad(inputs):
    sigma = jax.nn.sigmoid(inputs)
    return sigma * (1.0 + inputs * (1.0 - sigma))


def inverse_rms(inputs):
    return lax.rsqrt(jnp.mean(inputs * inputs, axis=-1, keepdims=True) + EPSILON)


def normalize_back(inputs, grad):
    factor = inverse_rms(inputs)
    normed = inputs * factor
    return factor * (grad - normed * jnp.mean(grad * normed, axis=-1, keepdims=True))


def first_half(shape):
    return lax.broadcasted_iota(jnp.int32, shape, len(shape) - 1) < HEAD_DIM


def head_parts(pair):
    low = first_half(pair.shape)
    zero = jnp.zeros_like(pair)
    return (jnp.where(low, pair, zero), jnp.where(low, zero, pair))


def compact(full):
    return jnp.where(first_half((HEAD_DIM, LANES)), full[:HEAD_DIM], full[HEAD_DIM:])


def expand(state):
    return jnp.concatenate(head_parts(state), axis=0)


def params(limit=56):
    return pltpu.CompilerParams(vmem_limit_bytes=limit * MIB)


def cost(flops, nbytes, share=0.1):
    return pl.CostEstimate(flops=int(flops / share), bytes_accessed=int(nbytes / share), transcendentals=0)


def whole(shape):
    return pl.BlockSpec(shape, lambda i: (0,) * len(shape))


def cols(rows, width=TILE):
    return pl.BlockSpec((rows, width), lambda i: (0, i))


def rows_of(rows, width=D):
    return pl.BlockSpec((rows, width), lambda i: (i, 0))


def exact(left, right, dims):
    return lax.dot_general(
        left, right, (dims, ((), ())), preferred_element_type=F32, precision=lax.Precision.HIGHEST
    )


def decay_kernel(log_ref, last_ref, cum_ref, lead_ref, trail_ref, mask_ref, mask_t_ref):
    logs = log_ref[...]
    length = logs.shape[1]
    row = lax.broadcasted_iota(jnp.int32, (length, length), 0)
    col = lax.broadcasted_iota(jnp.int32, (length, length), 1)
    cum = exact(logs, (row <= col).astype(F32), ((1,), (0,)))
    cum_ref[...] = cum
    last = cum[:, length - 1 :]
    last_ref[...] = last
    lane = lax.broadcasted_iota(jnp.int32, (HEAD_COUNT, D), 1) // HEAD_DIM
    spread = (lane == lax.broadcasted_iota(jnp.int32, (HEAD_COUNT, D), 0)).astype(F32)
    lead_ref[...] = jnp.exp(exact(cum, spread, ((0,), (0,))))
    trail_ref[...] = jnp.exp(exact(last - cum, spread, ((0,), (0,))))
    upright = cum.T
    for h in range(HEAD_COUNT):
        span = upright[:, h : h + 1] - cum[h : h + 1, :]
        mask_ref[h] = jnp.where(row >= col, jnp.exp(jnp.minimum(span, 0.0)), 0.0)
        mask_t_ref[h] = jnp.where(col >= row, jnp.exp(jnp.minimum(-span, 0.0)), 0.0)


def factor_kernel(members, place_ref, logs_ref, out_ref):
    logs = logs_ref[...]
    count = logs.shape[0]
    quad, member = place_ref[0], place_ref[1]
    here = quad * members + member
    start, end = quad * members, quad * members + members - 1
    row = lax.broadcasted_iota(jnp.int32, (count, count), 0)
    col = lax.broadcasted_iota(jnp.int32, (count, count), 1)
    before = exact((col < row).astype(F32), logs, ((1,), (0,)))
    through = before + logs
    at_row = lax.broadcasted_iota(jnp.int32, (count, HEAD_COUNT), 0)

    def at(sums, i):
        return jnp.sum(jnp.where(at_row == i, sums, 0.0), axis=0, keepdims=True)

    def factor(log, valid=True):
        return jnp.where(valid, jnp.exp(jnp.minimum(log, 0.0)), 0.0)

    rows = []
    for backward in (False, True):
        for k in range(1, QUADS):
            if backward:
                rows.append(factor(at(before, here + k * members) - at(through, end), quad + k < QUADS))
            else:
                rows.append(factor(at(before, start) - at(through, here - k * members), quad - k >= 0))
        spots = [lax.rem(member + k, members) for k in range(members)]
        for spot in spots:
            there = start + spot
            rows.append(factor(at(through, end) - at(through, there) if backward else at(before, there) - at(before, start)))
        for spot in spots:
            there = start + spot
            if backward:
                rows.append(factor(at(before, here) - at(through, there), spot < member))
            else:
                rows.append(factor(at(before, there) - at(through, here), spot > member))
    lane = lax.broadcasted_iota(jnp.int32, (HEAD_COUNT, D), 1) // HEAD_DIM
    spread = (lane == lax.broadcasted_iota(jnp.int32, (HEAD_COUNT, D), 0)).astype(F32)
    out_ref[...] = exact(jnp.concatenate(rows, axis=0), spread, ((1,), (0,)))


def kv_kernel(seqs, x_ref, w_ref, trail_ref, normed_ref, pk_ref, k_ref, v_ref, state_ref):
    @pl.when(pl.program_id(0) == 0)
    def _():
        inputs = x_ref[...].astype(F32)
        normed_ref[...] = (inputs * inverse_rms(inputs)).astype(BF16)

    normed = normed_ref[...]
    pre_k = dot_nn(normed, w_ref[0])
    keys = pre_k * jax.nn.sigmoid(pre_k)
    values = dot_nn(normed, w_ref[1]).astype(BF16)
    pk_ref[...] = pre_k.astype(BF16)
    k_ref[...] = keys.astype(BF16)
    v_ref[...] = values
    trail = trail_ref[...]
    length = trail.shape[0]
    for b in range(seqs):
        at = slice(b * length, (b + 1) * length)
        scaled = (keys[at] * trail).astype(BF16)
        for p in range(PAIRS_PER_TILE):
            lanes = slice(p * LANES, (p + 1) * LANES)
            state_ref[b, p] = compact(dot_tn(scaled[:, lanes], values[at, lanes])).astype(BF16)


def q_kernel(seqs, normed_ref, w_ref, k_ref, v_ref, mask_ref, pq_ref, q_ref, pg_ref, o_ref):
    normed = normed_ref[...]
    pre_q = dot_nn(normed, w_ref[0])
    pq_ref[...] = pre_q.astype(BF16)
    q_ref[...] = (pre_q * jax.nn.sigmoid(pre_q)).astype(BF16)
    pg_ref[...] = dot_nn(normed, w_ref[1]).astype(BF16)
    length = mask_ref.shape[1]
    for b in range(seqs):
        at = slice(b * length, (b + 1) * length)
        for p in range(PAIRS_PER_TILE):
            lanes = slice(p * LANES, (p + 1) * LANES)
            q_parts = head_parts(q_ref[at, lanes])
            v_parts = head_parts(v_ref[at, lanes])
            keys = k_ref[at, lanes]
            total = jnp.zeros((length, LANES), F32)
            for h in range(2):
                scores = dot_nt(q_parts[h], keys) * mask_ref[2 * p + h]
                total = total + dot_nn(scores.astype(BF16), v_parts[h])
            o_ref[at, lanes] = total


def mid_kernel(o_ref, q_ref, state_ref, lead_ref, pg_ref, x_ref, wo_ref, att_ref, hid_ref, mid_ref, nf_ref):
    scaled = (q_ref[...].astype(F32) * lead_ref[...]).astype(BF16)
    for p in range(PAIRS):
        lanes = slice(p * LANES, (p + 1) * LANES)
        att_ref[:, lanes] = o_ref[:, lanes] + dot_nn(scaled[:, lanes], expand(state_ref[0, p]))
    attended = att_ref[...]
    gate_in = pg_ref[...].astype(F32)
    hidden = (attended * inverse_rms(attended) * gate_in * jax.nn.sigmoid(gate_in)).astype(BF16)
    hid_ref[...] = hidden
    middle = x_ref[...].astype(F32) + dot_nn(hidden, wo_ref[...])
    mid_ref[...] = middle
    nf_ref[...] = (middle * inverse_rms(middle)).astype(BF16)


def ffn_kernel(carry, last, more, cut, place_ref, x_refs, out_refs, buffers, sems):
    nf_buf, cot_buf, w_in_buf, w_down_buf, out_buf, dn_buf, prod_buf, first_buf, second_buf, grad_buf = buffers[:10]
    rows = grad_buf.shape[1]
    if place_ref is None:
        targets = [nf_buf, w_in_buf, cot_buf, w_down_buf]
    else:
        half = rows // 2
        here = pl.ds(pl.multiple_of(place_ref[0] * half, half), half)
        there = pl.ds(pl.multiple_of((1 - place_ref[0]) * half, half), half)
        targets = [nf_buf, w_in_buf.at[:, here], w_in_buf.at[:, there], cot_buf, w_down_buf.at[here], w_down_buf.at[there]]
    needed = len(targets)
    targets = targets + [out_buf, dn_buf][:carry] + ([grad_buf] if more else [])
    loads = [
        pltpu.make_async_copy(source, target, sems.at[i]) for i, (source, target) in enumerate(zip(x_refs, targets))
    ]
    for load in loads:
        load.start()
    sum_bufs = buffers[10:] if last else (out_buf, dn_buf)
    out_copies = [pltpu.make_async_copy(buf, ref, sems.at[9 + i]) for i, (buf, ref) in enumerate(zip(sum_bufs, out_refs))]
    pieces = [pl.ds(0, cut), pl.ds(cut, rows - cut)] if cut else [pl.ds(0, rows)]
    grad_copies = [
        [
            pltpu.make_async_copy(grad_buf.at[i, piece], out_refs[2 + j].at[i], sems.at[11 + 2 * i + j])
            for j, piece in enumerate(pieces)
        ]
        for i in range(3)
    ]
    count = nf_buf.shape[0]
    first_half = 2 if place_ref is None else 3
    step = min(TILE, count)
    for at in [slice(t, t + step) for t in range(0, count, step)]:
        if at.start == 0:
            for load in loads[:first_half]:
                load.wait()
        normed = nf_buf[at, :]
        first = dot_nt(w_in_buf[0], normed)
        second = dot_nt(w_in_buf[1], normed)
        if at.start == 0:
            for load in loads[first_half:needed]:
                load.wait()
        cot = cot_buf[at, :]
        d_product = dot_nt(w_down_buf[...], cot)
        product = (first * second).astype(BF16)
        d_first = (d_product * second).astype(BF16)
        d_second = (d_product * first).astype(BF16)
        prod_buf[:, at] = product
        first_buf[:, at] = d_first
        second_buf[:, at] = d_second
        out = dot_tn(product, w_down_buf[...])
        d_normed = dot_tn(d_first, w_in_buf[0]) + dot_tn(d_second, w_in_buf[1])
        if at.start == 0:
            for load in loads[needed:]:
                load.wait()
        if carry > 0:
            out = out_buf[at, :] + out
        if carry > 1:
            d_normed = dn_buf[at, :] + d_normed
        sum_bufs[0][at, :] = out.astype(sum_bufs[0].dtype)
        sum_bufs[1][at, :] = d_normed.astype(sum_bufs[1].dtype)
    for copy in out_copies:
        copy.start()
    for i, (left, right) in enumerate(((first_buf, nf_buf), (second_buf, nf_buf), (prod_buf, cot_buf))):
        for at in [slice(c, c + TILE) for c in range(0, D, TILE)]:
            grad = dot_nn(left[...], right[:, at])
            if more:
                grad = grad + grad_buf[i, :, at].astype(F32)
            grad_buf[i, :, at] = grad.astype(BF16)
        for copy in grad_copies[i]:
            copy.start()
    for copy in out_copies + [copy for copies in grad_copies for copy in copies]:
        copy.wait()


def ffn(normed, cot, weights, sums=(), last=False, grads=None, cut=0, place=None):
    w_in, w_down = ((w,) if place is None else w for w in weights)
    count, rows = normed.shape[0], sum(part.shape[0] for part in w_down)
    away = pl.BlockSpec(memory_space=pl.ANY)
    kind = BF16 if last else F32
    ins = (normed, *w_in, cot, *w_down, *sums) + (() if grads is None else (grads,))
    places = () if place is None else (place,)
    n_in = len(ins)
    parts = [cut, rows - cut] if cut else [rows]
    n_out = 2 + len(parts)
    has_grads = grads is not None

    def body(*refs):
        place_ref = refs[0] if places else None
        refs = refs[len(places) :]
        outs, buffers = refs[n_in : n_in + n_out], refs[n_in + n_out : -1]
        ffn_kernel(len(sums), last, has_grads, cut, place_ref, refs[:n_in], outs, buffers, refs[-1])

    tokens_by = pltpu.VMEM((count, D), BF16)
    units_by = pltpu.VMEM((rows, count), BF16)
    out, d_normed, *grads = pl.pallas_call(
        body,
        in_specs=[pl.BlockSpec(memory_space=pltpu.SMEM)] * len(places) + [away] * n_in,
        out_specs=[away] * n_out,
        out_shape=[jax.ShapeDtypeStruct((count, D), kind)] * 2
        + [jax.ShapeDtypeStruct((3, part, D), BF16) for part in parts],
        scratch_shapes=[tokens_by, tokens_by, pltpu.VMEM((2, rows, D), BF16), pltpu.VMEM((rows, D), BF16)]
        + [pltpu.VMEM((count, D), F32)] * 2
        + [units_by] * 3
        + [pltpu.VMEM((3, rows, D), BF16)]
        + ([tokens_by] * 2 if last else [])
        + [pltpu.SemaphoreType.DMA((17,))],
        compiler_params=params(60),
        cost_estimate=cost(16 * count * D * rows, 12 * rows * D + 12 * count * D),
        name="ffn",
    )(*places, *ins)
    return (out, d_normed), grads


def gate_back_kernel(
    dn_ref, dn_mate_ref, mid_ref, cot_ref, wo_ref, att_ref, pg_ref, q_ref, lead_ref, *out_refs
):
    dmid_ref, datt_ref, dgate_ref, state_ref = out_refs
    d_normed_ffn = dn_ref[...] + dn_mate_ref[...].astype(F32)
    d_middle = cot_ref[...].astype(F32) + normalize_back(mid_ref[...], d_normed_ffn)
    d_middle = d_middle.astype(BF16)
    dmid_ref[...] = d_middle
    d_hidden = dot_nt(d_middle, wo_ref[...])
    attended = att_ref[...]
    factor = inverse_rms(attended)
    out_norm = attended * factor
    gate_in = pg_ref[...].astype(F32)
    sigma = jax.nn.sigmoid(gate_in)
    dgate_ref[...] = (d_hidden * out_norm * sigma * (1.0 + gate_in * (1.0 - sigma))).astype(BF16)
    grad = d_hidden * gate_in * sigma
    d_att = factor * (grad - out_norm * jnp.mean(grad * out_norm, axis=-1, keepdims=True))
    d_att = d_att.astype(BF16)
    datt_ref[...] = d_att
    scaled = (q_ref[...].astype(F32) * lead_ref[...]).astype(BF16)
    for p in range(PAIRS):
        lanes = slice(p * LANES, (p + 1) * LANES)
        state_ref[0, p] = compact(dot_tn(scaled[:, lanes], d_att[:, lanes])).astype(BF16)


def early_grads_kernel(hid_ref, nf_ref, dmid_ref, dgate_ref, out_grad_ref, gate_grad_ref):
    out_grad_ref[0] = dot_tn(hid_ref[...], dmid_ref[...]).astype(BF16)
    gate_grad_ref[0] = dot_tn(nf_ref[...], dgate_ref[...]).astype(BF16)


def att_back_kernel(
    seqs, q_ref, k_ref, v_ref, da_ref, pq_ref, mask_ref, mask_t_ref, state_ref, lead_ref, nf_ref, *out_refs
):
    dq_ref, dk_ref, dv_ref, grad_ref = out_refs[1:]
    lead = lead_ref[...]
    length = lead.shape[0]
    for b in range(seqs):
        at = slice(b * length, (b + 1) * length)
        for p in range(PAIRS_PER_TILE):
            lanes = slice(p * LANES, (p + 1) * LANES)
            queries, keys, values, d_att = (r[at, lanes] for r in (q_ref, k_ref, v_ref, da_ref))
            q_parts, k_parts, v_parts, d_parts = (head_parts(a) for a in (queries, keys, values, d_att))
            d_q = dot_nt((d_att.astype(F32) * lead[:, lanes]).astype(BF16), expand(state_ref[b, p]))
            d_k = jnp.zeros((length, LANES), F32)
            d_v = jnp.zeros((length, LANES), F32)
            for h in range(2):
                mask, mask_t = mask_ref[2 * p + h], mask_t_ref[2 * p + h]
                d_scores = (dot_nt(d_parts[h], values) * mask).astype(BF16)
                d_scores_t = (dot_nt(v_parts[h], d_att) * mask_t).astype(BF16)
                scores_t = (dot_nt(k_parts[h], queries) * mask_t).astype(BF16)
                d_q = d_q + dot_nn(d_scores, k_parts[h])
                d_k = d_k + dot_nn(d_scores_t, q_parts[h])
                d_v = d_v + dot_nn(scores_t, d_parts[h])
            dq_ref[at, lanes] = (d_q * silu_grad(pq_ref[at, lanes].astype(F32))).astype(BF16)
            dk_ref[at, lanes] = d_k
            dv_ref[at, lanes] = d_v
    grad_ref[0] = dot_tn(nf_ref[...], dq_ref[...]).astype(BF16)


def state_back_kernel(
    seqs, k_ref, v_ref, pk_ref, dk_in_ref, dv_in_ref, state_ref, trail_ref, nf_ref, _, dkv_ref, grad_ref
):
    trail = trail_ref[...]
    length = trail.shape[0]
    for b in range(seqs):
        at = slice(b * length, (b + 1) * length)
        k_scaled = (k_ref[at, :].astype(F32) * trail).astype(BF16)
        v_scaled = (v_ref[at, :].astype(F32) * trail).astype(BF16)
        for p in range(PAIRS_PER_TILE):
            lanes = slice(p * LANES, (p + 1) * LANES)
            state = expand(state_ref[b, p])
            d_k = dk_in_ref[at, lanes] + dot_nt(v_scaled[:, lanes], state)
            d_v = dv_in_ref[at, lanes] + dot_nn(k_scaled[:, lanes], state)
            dkv_ref[0, at, lanes] = (d_k * silu_grad(pk_ref[at, lanes].astype(F32))).astype(BF16)
            dkv_ref[1, at, lanes] = d_v.astype(BF16)
    for i in range(2):
        grad_ref[i] = dot_tn(nf_ref[...], dkv_ref[i]).astype(BF16)


def dots_back_kernel(dq_ref, dg_ref, w_ref, out_ref):
    out_ref[...] = dot_nt(dq_ref[...], w_ref[0]) + dot_nt(dg_ref[...], w_ref[1])


def input_back_kernel(dkv_ref, w_ref, part_ref, x_ref, dmid_ref, out_ref):
    d_normed = part_ref[...] + dot_nt(dkv_ref[0], w_ref[0]) + dot_nt(dkv_ref[1], w_ref[1])
    d_tokens = dmid_ref[...].astype(F32) + normalize_back(x_ref[...].astype(F32), d_normed)
    out_ref[...] = d_tokens.astype(BF16)


def newton_kernel(parts, *refs):
    b_refs, (row_ref, out_ref, rest_ref, g_ref, gb_ref, nb_ref, h_ref, hb_ref, x_ref) = refs[:parts], refs[parts:]
    tiles = [slice(i * TILE, (i + 1) * TILE) for i in range(D // TILE)]

    def right_of(at):
        return slice(at.start, D)

    def mirrored(target, at, part):
        low = part.astype(BF16)
        target[at, right_of(at)] = low
        for other in tiles:
            if other.start > at.start:
                target[other, at] = low[:, other.start - at.start : other.stop - at.start].T

    trace = jnp.zeros((1, 1), F32)
    for at in tiles:
        part = sum(dot_tn(b_ref[:, at], b_ref[:, right_of(at)]) for b_ref in b_refs)
        g_ref[at, right_of(at)] = part
        on_row = lax.broadcasted_iota(jnp.int32, (TILE, TILE), 0)
        on_col = lax.broadcasted_iota(jnp.int32, (TILE, TILE), 1)
        trace = trace + jnp.sum(jnp.where(on_row == on_col, part[:, :TILE], 0.0), keepdims=True)
    inverse = 1.0 / (jnp.sqrt(trace) + NORM_FLOOR)
    x_ref[...] = row_ref[...].astype(F32) * inverse
    scale = inverse * inverse
    for at in tiles:
        gram = g_ref[at, right_of(at)] * scale
        g_ref[at, right_of(at)] = gram
        mirrored(gb_ref, at, gram)

    def polynomial():
        for at in tiles:
            square = dot_nn(gb_ref[at, :], gb_ref[:, right_of(at)])
            mirrored(nb_ref, at, COEFF_B * g_ref[at, right_of(at)] + COEFF_C * square)
        state = x_ref[...]
        x_ref[...] = COEFF_A * state + dot_nn(state.astype(BF16), nb_ref[...])

    @pl.loop(0, ITERS - 1)
    def _(turn):
        polynomial()
        for at in tiles:
            half = COEFF_A * g_ref[at, right_of(at)] + dot_nn(gb_ref[at, :], nb_ref[:, right_of(at)])
            h_ref[at, right_of(at)] = half
            mirrored(hb_ref, at, half)
        for at in tiles:
            gram = COEFF_A * h_ref[at, right_of(at)] + dot_nn(nb_ref[at, :], hb_ref[:, right_of(at)])
            g_ref[at, right_of(at)] = gram
            mirrored(gb_ref, at, gram)

    polynomial()
    own = out_ref.shape[0]
    out_ref[...] = x_ref[:own, :].astype(BF16)
    rest_ref[...] = x_ref[own:, :].astype(BF16)


def newton_rows(every, mine, first):
    rows, own = sum(part.shape[0] for part in every), mine.shape[0]
    return pl.pallas_call(
        lambda *refs: newton_kernel(len(every), *refs),
        out_shape=[jax.ShapeDtypeStruct((first, D), BF16), jax.ShapeDtypeStruct((own - first, D), BF16)],
        grid=(1,),
        in_specs=[whole(part.shape) for part in every] + [whole((own, D))],
        out_specs=[whole((first, D)), whole((own - first, D))],
        scratch_shapes=[
            pltpu.VMEM((D, D), F32),
            pltpu.VMEM((D, D), BF16),
            pltpu.VMEM((D, D), BF16),
            pltpu.VMEM((D, D), F32),
            pltpu.VMEM((D, D), BF16),
            pltpu.VMEM((own, D), F32),
        ],
        compiler_params=params(),
        cost_estimate=cost(2 * D * D * (13 * D + rows + 5 * own), 2 * D * (rows + 2 * own)),
        name="newton",
    )(*every, mine)


class Places:
    def __init__(self):
        self.members = lax.axis_size("seq") // QUADS
        self.chips = lax.axis_size("batch") // 2
        at = lax.axis_index("seq").astype(jnp.uint32)
        self.quad, self.member = at // self.members, at % self.members
        at = lax.axis_index("batch").astype(jnp.uint32)
        self.chip, self.core = at // 2, at % 2

    def level(self, name):
        return {
            "quads": (QUADS, self.quad),
            "members": (self.members, self.member),
            "chips": (self.chips, self.chip),
            "core": (2, self.core),
        }[name]

    def send(self, value, name, k, wrap=True):
        pairs = []
        if name in ("quads", "members"):
            for q in range(QUADS):
                for m in range(self.members):
                    if name == "members":
                        pairs.append((q * self.members + m, q * self.members + (m + k) % self.members))
                    elif wrap or 0 <= q + k < QUADS:
                        pairs.append((q * self.members + m, (q + k) % QUADS * self.members + m))
            return lax.ppermute(value, "seq", pairs)
        for x in range(self.chips):
            for c in range(2):
                to = 2 * x + (c + k) % 2 if name == "core" else (x + k) % self.chips * 2 + c
                pairs.append((2 * x + c, to))
        return lax.ppermute(value, "batch", pairs)

    def pair(self, value):
        pairs = []
        for q in range(QUADS):
            for m in range(self.members):
                pairs.append((q * self.members + m, (q ^ 1) * self.members + m))
        return lax.ppermute(value, "seq", pairs)

    def scattered(self, blocks, name, axis=0):
        count, mine = self.level(name)

        def block(j):
            return lax.dynamic_index_in_dim(blocks, j, axis, False)

        return [block(mine)] + [self.send(block((mine + k) % count), name, k) for k in range(1, count)]

    def scatter(self, blocks, name, axis=0):
        return summed(*self.scattered(blocks, name, axis)).astype(BF16)

    def gather(self, block, name, axis=0):
        count, mine = self.level(name)
        shape = block.shape[:axis] + (count,) + block.shape[axis:]
        result = jnp.zeros(shape, block.dtype)
        result = lax.dynamic_update_index_in_dim(result, block, mine, axis)
        for k in range(1, count):
            part = self.send(block, name, k)
            result = lax.dynamic_update_index_in_dim(result, part, (mine + (count - k)) % count, axis)
        return result

    def far_rows(self, own, after, pair_after, use_after):
        n, rows, _ = own.shape
        split = own.reshape(n, 2, rows // 2, D)
        mine = tied(lax.dynamic_index_in_dim(split, self.quad % 2, 1, False), after)
        far = []
        for k in range(1, self.chips):
            part = tied(self.send(mine, "chips", k), pair_after)
            far.append(tied((part, self.pair(part)), use_after))
        return far


def tied(value, *others):
    return lax.optimization_barrier((value, others))[0]


class Carried:
    def __init__(self, places, local, factors, backward):
        self.places = places
        factors = factors.reshape(-1, PAIRS, 1, LANES)
        self.quad_factors = factors[: QUADS - 1]
        self.spot_factors = factors[QUADS - 1 : QUADS - 1 + places.members]
        self.local_factors = factors[QUADS - 1 + places.members :]
        self.local = local
        sign = -1 if backward else 1
        self.arrived = [places.send(self.local, "quads", sign * k, wrap=False) for k in range(1, QUADS)]

    def finish(self, after=()):
        outer = sum(part.astype(F32) * self.quad_factors[k] for k, part in enumerate(self.arrived))
        local = self.local.astype(F32)
        own = self.spot_factors[0] * outer
        self.sent = [
            tied((self.spot_factors[k] * outer + self.local_factors[k] * local).astype(BF16), after)
            for k in range(1, self.places.members)
        ]
        parts = [self.places.send(part, "members", k) for k, part in enumerate(self.sent, 1)]
        return summed(own, *parts).astype(BF16)


def padded(block, rows):
    return jnp.pad(block, ((0, rows - block.shape[0]), (0, 0)))


def summed(*parts):
    total = parts[0].astype(F32)
    for part in parts[1:]:
        total = total + part.astype(F32)
    return total


class WideSum:
    def __init__(self, places, rows):
        self.places = places
        self.shape = (3, places.members, rows // places.members, D)

    def ordered(self, weights):
        places = self.places
        split = weights.reshape(weights.shape[0], places.members, -1, D)
        parts = [
            lax.dynamic_index_in_dim(split, (places.member + k) % places.members, 1, False)
            for k in range(places.members)
        ]
        return jnp.concatenate(parts, axis=1).astype(BF16)

    def cut(self):
        own = self.shape[2]
        return own if own % 16 == 0 else 0

    def parts(self, grads):
        if len(grads) == 1:
            split = grads[0].reshape(self.shape)
            return split[:, 0], [split[:, k] for k in range(1, self.places.members)]
        split = grads[1].reshape((3, -1) + self.shape[2:])
        if self.places.members == 2:
            return grads[0], [grads[1]]
        return grads[0], [split[:, k] for k in range(self.places.members - 1)]

    def exchange(self, offers):
        return [self.places.send(offer, "members", k + 1) for k, offer in enumerate(offers)]


def place_kernel(members, rows, sources, place_ref, *refs):
    sources_refs, out_ref, sems = refs[:-2], refs[-2], refs[-1]
    quad, member = place_ref[0], place_ref[1]
    copies = []
    for i, (ref, start, k, j) in enumerate(sources):
        q, m = lax.rem(quad + (QUADS - k), QUADS), lax.rem(member + (members - j), members)
        block = sources_refs[ref].at[pl.ds(start, rows)]
        copies.append(pltpu.make_async_copy(block, out_ref.at[q, m], sems.at[i]))
    for copy in copies:
        copy.start()
    for copy in copies:
        copy.wait()


def finish_kernel(members, sources, groups, scales, copies, place_ref, *refs):
    count = len({array for array, _, _ in groups})
    n_blocks = len({ref for ref, _, _, _ in sources})
    block_refs, refs = refs[:n_blocks], refs[n_blocks:]
    base_refs, refs = refs[:count], refs[count:]
    out_refs, refs = refs[:count], refs[count:]
    if copies:
        low_refs, refs = refs[:count], refs[count:]
        block_buf, base_buf, low_buf, sems = refs
    else:
        block_buf, base_buf, sems = refs
    quad, member = place_ref[0], place_ref[1]
    rows = block_buf.shape[2]
    loads = []
    for i, (ref, start, k, j) in enumerate(sources):
        q, m = lax.rem(quad + (QUADS - k), QUADS), lax.rem(member + (members - j), members)
        block = block_refs[ref].at[pl.ds(start, rows)]
        loads.append(pltpu.make_async_copy(block, block_buf.at[q, m], sems.at[0, i]))

    def whole_of(ref, q):
        array, at, _ = groups[q]
        return ref[array] if at is None else ref[array].at[at]

    def used(buf, q):
        return buf.at[q, pl.ds(0, members * groups[q][2])]

    bases = [pltpu.make_async_copy(whole_of(base_refs, q), used(base_buf, q), sems.at[1, q]) for q in range(QUADS)]
    for copy in loads + bases:
        copy.start()
    for copy in loads:
        copy.wait()
    stores = []
    for q in range(QUADS):
        bases[q].wait()
        own = groups[q][2]
        for m in range(members):
            at = slice(m * own, (m + 1) * own)
            value = scales[0] * base_buf[q, at] + scales[1][q] * block_buf[q, m, :own].astype(F32)
            base_buf[q, at] = value
            if copies:
                low_buf[q, at] = value.astype(BF16)
        store = [pltpu.make_async_copy(used(base_buf, q), whole_of(out_refs, q), sems.at[2, q])]
        if copies:
            store.append(pltpu.make_async_copy(used(low_buf, q), whole_of(low_refs, q), sems.at[3, q]))
        for copy in store:
            copy.start()
        stores += store
    for copy in stores:
        copy.wait()


class Blocks:
    def __init__(self, places, rows):
        self.places, self.rows = places, rows
        self.arrays, self.sources = [], []

    def add(self, array, *blocks):
        whole_tiles = all(n % 16 == 0 for n in (self.rows, *(start for start, _, _ in blocks)))
        for start, k, j in blocks:
            self.sources.append((len(self.arrays), start if whole_tiles else 0, k, j))
            if not whole_tiles:
                self.arrays.append(array[start : start + self.rows])
        if whole_tiles:
            self.arrays.append(array)

    def finished(self, arrays, groups, scales, copies=False, late=()):
        places = self.places
        away = pl.BlockSpec(memory_space=pl.ANY)
        outs = [jax.ShapeDtypeStruct(array.shape, F32) for array in arrays]
        lows = [jax.ShapeDtypeStruct(array.shape, BF16) for array in arrays] if copies else []
        if any(own % 16 for _, _, own in groups):
            blocks = self.placed(late)
            parts = [blocks[q, :, :own].reshape(-1, D).astype(F32) * scales[1][q] for q, (_, _, own) in enumerate(groups)]
            results = []
            for i, array in enumerate(arrays):
                mine = [part for part, (at, _, _) in zip(parts, groups) if at == i]
                results.append(scales[0] * array + jnp.stack(mine).reshape(array.shape))
            return results + [result.astype(BF16) for result in results if copies]
        tall = (QUADS, places.members * self.rows, D)
        return pl.pallas_call(
            lambda *refs: finish_kernel(places.members, self.sources, groups, scales, copies, *refs),
            in_specs=[pl.BlockSpec(memory_space=pltpu.SMEM)] + [away] * (len(self.arrays) + len(arrays)),
            out_specs=[away] * (len(outs) + len(lows)),
            out_shape=outs + lows,
            scratch_shapes=[
                pltpu.VMEM((QUADS, places.members, self.rows, D), BF16),
                pltpu.VMEM(tall, F32),
            ]
            + ([pltpu.VMEM(tall, BF16)] if copies else [])
            + [pltpu.SemaphoreType.DMA((4, len(self.sources)))],
            compiler_params=params(),
            name="finish",
        )(jnp.stack([places.quad, places.member]).astype(jnp.int32), *tied(self.arrays, late), *arrays)

    def placed(self, late=()):
        places = self.places
        away = pl.BlockSpec(memory_space=pl.ANY)
        return pl.pallas_call(
            lambda *refs: place_kernel(places.members, self.rows, self.sources, *refs),
            in_specs=[pl.BlockSpec(memory_space=pltpu.SMEM)] + [away] * len(self.arrays),
            out_specs=pl.BlockSpec(memory_space=pltpu.VMEM),
            out_shape=jax.ShapeDtypeStruct((QUADS, places.members, self.rows, D), BF16),
            scratch_shapes=[pltpu.SemaphoreType.DMA((len(self.sources),))],
            compiler_params=params(),
            name="place",
        )(jnp.stack([places.quad, places.member]).astype(jnp.int32), *tied(self.arrays, late))


def own_rows(places, sources, most):
    result = None
    zero = jnp.uint32(0)
    for i, (source, at) in enumerate(sources):
        rows = source.shape[1] // places.members
        part = lax.dynamic_slice(source, (jnp.uint32(at), places.member * rows, zero), (1, rows, D))[0]
        part = padded(part, most)
        result = part if result is None else jnp.where(places.quad == i, part, result)
    return result


def shards(tokens, cotangent, log_decay, w_mix, w_out, w_in, w_down, m_mix, m_out, m_in, m_down):
    places = Places()
    seqs, length, _ = tokens.shape
    count = seqs * length
    state_shape = (seqs, PAIRS, HEAD_DIM, LANES)
    tiles = D // TILE

    cot = cotangent.reshape(count, D)

    def gathered(*rows):
        return lax.all_gather(jnp.stack(rows).astype(BF16), "batch", axis=1, tiled=True)

    full_kv = gathered(w_mix[1], w_mix[2])
    full_qg = gathered(w_mix[0], w_mix[3])
    full_out = gathered(w_out)[0]
    square = jax.ShapeDtypeStruct((HEAD_COUNT, length, length), F32)
    by_lane = jax.ShapeDtypeStruct((length, D), F32)
    last, _, lead, trail, mask, mask_t = pl.pallas_call(
        decay_kernel,
        out_shape=[
            jax.ShapeDtypeStruct((HEAD_COUNT, 1), F32),
            jax.ShapeDtypeStruct((HEAD_COUNT, length), F32),
            by_lane,
            by_lane,
            square,
            square,
        ],
        compiler_params=params(),
        name="decay",
    )(log_decay)
    decays = places.gather(places.gather(last[:, 0], "members"), "quads").reshape(-1, HEAD_COUNT)
    members = places.members
    factors = pl.pallas_call(
        lambda *refs: factor_kernel(members, *refs),
        in_specs=[pl.BlockSpec(memory_space=pltpu.SMEM), pl.BlockSpec(memory_space=pltpu.VMEM)],
        out_shape=jax.ShapeDtypeStruct((2 * (2 * members + QUADS - 1), D), F32),
        compiler_params=params(),
        name="factors",
    )(jnp.stack([places.quad, places.member]).astype(jnp.int32), decays).reshape(2, -1, D)

    x = tokens.reshape(count, D)

    tile_state = pl.BlockSpec((seqs, PAIRS_PER_TILE, HEAD_DIM, LANES), lambda i: (0, i, 0, 0))
    row_state = pl.BlockSpec((1, PAIRS, HEAD_DIM, LANES), lambda i: (i, 0, 0, 0))
    tile_mask = pl.BlockSpec((HEADS_PER_TILE, length, length), lambda i: (i, 0, 0))
    pair_cols = pl.BlockSpec((2, D, TILE), lambda i: (0, 0, i))
    wide = jax.ShapeDtypeStruct((count, D), F32)
    narrow = jax.ShapeDtypeStruct((count, D), BF16)

    normed, pre_k, keys, values, summary = pl.pallas_call(
        lambda *refs: kv_kernel(seqs, *refs),
        grid=(tiles,),
        in_specs=[whole((count, D)), pair_cols, cols(length)],
        out_specs=[whole((count, D)), cols(count), cols(count), cols(count), tile_state],
        out_shape=[narrow, narrow, narrow, narrow, jax.ShapeDtypeStruct(state_shape, BF16)],
        compiler_params=params(),
        cost_estimate=cost(4 * count * D * D, 16 * count * D),
        name="kv",
    )(x, full_kv, trail)
    ahead = Carried(places, summary, factors[0], False)
    incoming = ahead.finish()

    cot_mate = places.send(tied(cot, full_kv), "core", 1)
    wide_sum = WideSum(places, w_down.shape[0])
    w_in_late, w_down_late = tied((w_in, w_down), full_kv)
    in_low, down_low = wide_sum.ordered(w_in_late), wide_sum.ordered(w_down_late[None])[0]

    pre_q, queries, gate_in, inner = pl.pallas_call(
        lambda *refs: q_kernel(seqs, *refs),
        grid=(tiles,),
        in_specs=[whole((count, D)), pair_cols, cols(count), cols(count), tile_mask],
        out_specs=[cols(count)] * 4,
        out_shape=[narrow, narrow, narrow, wide],
        compiler_params=params(),
        cost_estimate=cost(8 * count * D * D, 16 * count * D),
        name="query",
    )(normed, full_qg, keys, values, mask)

    attended, hidden, middle, normed_ffn = pl.pallas_call(
        mid_kernel,
        grid=(seqs,),
        in_specs=[
            rows_of(length),
            rows_of(length),
            row_state,
            whole((length, D)),
            rows_of(length),
            rows_of(length),
            whole((D, D)),
        ],
        out_specs=[rows_of(length)] * 4,
        out_shape=[wide, narrow, wide, narrow],
        compiler_params=params(),
        cost_estimate=cost(2 * count * D * D, 24 * count * D),
        name="middle",
    )(inner, queries, incoming, lead, gate_in, x, full_out)

    nf_mate = places.send(normed_ffn, "core", 1)
    near_weights = (in_low, down_low)
    sums, near_own = ffn(normed_ffn, cot, near_weights, (middle,))
    nf_mate, cot_mate = tied((nf_mate, cot_mate), sums)
    cut = wide_sum.cut()
    mate_sums, near = ffn(nf_mate, cot_mate, near_weights, grads=near_own[0], cut=cut)
    far_down = places.far_rows(down_low[None], full_qg, normed_ffn, mate_sums)
    far_in = places.far_rows(in_low, queries, sums, mate_sums)
    far_weights = [(part, [half[0] for half in down]) for part, down in zip(far_in, far_down)]
    place = (places.quad % 2).astype(jnp.int32).reshape(1)
    near, near_offers = wide_sum.parts(near)
    near_arrived = wide_sum.exchange(near_offers)
    far = []
    for k, weights in enumerate(far_weights):
        mate_sums = tied(mate_sums, near_offers)
        mate_sums, grad = ffn(nf_mate, cot_mate, weights, mate_sums, k == len(far_weights) - 1, place=place)
        far += grad
    out_mate, dn_mate = mate_sums
    dn_mate = places.send(dn_mate, "core", 1)
    for k, weights in enumerate(far_weights):
        sums, far[k] = ffn(normed_ffn, cot, weights, tied(sums, mate_sums), grads=far[k], cut=cut, place=place)
    far = [wide_sum.parts(grads) for grads in far]
    far_arrived = [wide_sum.exchange(offers) for _, offers in far]

    d_middle, d_attended, d_gate, local_grad = pl.pallas_call(
        gate_back_kernel,
        grid=(seqs,),
        in_specs=[
            rows_of(length),
            rows_of(length),
            rows_of(length),
            rows_of(length),
            whole((D, D)),
            rows_of(length),
            rows_of(length),
            rows_of(length),
            whole((length, D)),
        ],
        out_specs=[rows_of(length), rows_of(length), rows_of(length), row_state],
        out_shape=[narrow, narrow, narrow, jax.ShapeDtypeStruct(state_shape, BF16)],
        compiler_params=params(),
        cost_estimate=cost(2 * count * D * D, 16 * count * D),
        name="gate_back",
    )(sums[1], dn_mate, middle, cot, full_out, attended, gate_in, queries, lead)
    behind = Carried(places, local_grad, factors[1], True)
    one_cols = pl.BlockSpec((1, D, TILE), lambda i: (0, 0, i))
    four_grads = jax.ShapeDtypeStruct((4, D, D), BF16)
    out_grad, mix_grads = pl.pallas_call(
        early_grads_kernel,
        grid=(tiles,),
        in_specs=[whole((count, D)), whole((count, D)), cols(count), cols(count)],
        out_specs=[one_cols, pl.BlockSpec((1, D, TILE), lambda i: (3, 0, i))],
        out_shape=[jax.ShapeDtypeStruct((1, D, D), BF16), four_grads],
        compiler_params=params(),
        cost_estimate=cost(4 * count * D * D, 12 * count * D),
        name="early_grads",
    )(hidden, normed, d_middle, d_gate)
    d_attended = tied(d_attended, near_arrived)
    d_query, d_key_part, d_value_part, mix_grads = pl.pallas_call(
        lambda *refs: att_back_kernel(seqs, *refs),
        grid=(tiles,),
        in_specs=[cols(count)] * 5
        + [tile_mask, tile_mask, tile_state, cols(length), whole((count, D)), pl.BlockSpec(memory_space=pl.ANY)],
        out_specs=[cols(count)] * 3 + [pl.BlockSpec((1, D, TILE), lambda i: (2, 0, i))],
        out_shape=[narrow, wide, wide, four_grads],
        input_output_aliases={10: 3},
        compiler_params=params(),
        cost_estimate=cost(8 * count * D * D, 20 * count * D),
        name="attention_back",
    )(queries, keys, values, d_attended, pre_q, mask, mask_t, incoming, lead, normed, mix_grads)

    def scattered(grads):
        return lax.psum_scatter(grads, "batch", scatter_dimension=1, tiled=True)

    def members_sum(grads):
        n, rows, _ = grads.shape
        return places.scatter(grads.reshape(n, places.members, rows // places.members, D), "members", 1)

    sum_out = scattered(out_grad)
    far_sums = [
        tied(summed(own, *arrived).astype(BF16), d_query) for (own, _), arrived in zip(far, far_arrived)
    ]
    chip_arrived = [places.send(part, "chips", -(k + 1)) for k, part in enumerate(far_sums)]
    outgoing = behind.finish((d_query, far_sums, sum_out))
    out_mate = places.send(tied(out_mate, d_query), "core", 1)
    sum_out = members_sum(tied(sum_out, behind.sent))[0]
    outgoing = tied(outgoing, sum_out)
    d_normed_part = pl.pallas_call(
        dots_back_kernel,
        grid=(seqs,),
        in_specs=[rows_of(length), rows_of(length), whole((2, D, D))],
        out_specs=rows_of(length),
        out_shape=wide,
        compiler_params=params(),
        cost_estimate=cost(4 * count * D * D, 10 * count * D),
        name="normed_back",
    )(*tied((d_query, d_gate), behind.sent), full_qg)
    outgoing = tied(outgoing, d_normed_part)

    d_kv, mix_grads = pl.pallas_call(
        lambda *refs: state_back_kernel(seqs, *refs),
        grid=(tiles,),
        in_specs=[cols(count)] * 5
        + [tile_state, cols(length), whole((count, D)), pl.BlockSpec(memory_space=pl.ANY)],
        out_specs=[pl.BlockSpec((2, count, TILE), lambda i: (0, 0, i)), pair_cols],
        out_shape=[jax.ShapeDtypeStruct((2, count, D), BF16), four_grads],
        input_output_aliases={8: 1},
        compiler_params=params(),
        cost_estimate=cost(5 * count * D * D, 18 * count * D),
        name="state_back",
    )(keys, values, pre_k, d_key_part, d_value_part, outgoing, trail, normed, mix_grads)
    wide_total = summed(near, *near_arrived, *chip_arrived).astype(BF16)
    sum_out = padded(sum_out, w_down.shape[0] // places.members)
    wide_blocks = jnp.stack([wide_total[2], wide_total[0], wide_total[1], sum_out])
    wide_parts = places.scattered(wide_blocks, "quads")
    mix_sums = scattered(tied(mix_grads, chip_arrived))
    activations = (tied(sums[0], wide_blocks) + out_mate.astype(F32)).astype(BF16)
    d_kv = tied(d_kv, wide_blocks)

    input_grad = pl.pallas_call(
        input_back_kernel,
        grid=(seqs,),
        in_specs=[
            pl.BlockSpec((2, length, D), lambda i: (0, i, 0)),
            whole((2, D, D)),
            rows_of(length),
            rows_of(length),
            rows_of(length),
        ],
        out_specs=rows_of(length),
        out_shape=narrow,
        compiler_params=params(),
        cost_estimate=cost(4 * count * D * D, 16 * count * D),
        name="input_back",
    )(d_kv, full_kv, d_normed_part, x, d_middle).reshape(tokens.shape)

    wide_mom = ((m_down[None], 0), (m_in, 0), (m_in, 1), (m_out[None], 0))
    mix_mom = [(m_mix, i) for i in range(4)]

    def momentum_rows(sources, grad, after):
        arrays = tied([array for array, _ in sources], after)
        own = own_rows(places, [(array, at) for array, (_, at) in zip(arrays, sources)], grad.shape[0])
        return (MOMENTUM * own + grad.astype(F32)).astype(BF16)

    def to_members(part):
        return [places.send(part, "members", j) for j in range(1, places.members)]

    mix_split = tied(mix_sums, (input_grad, wide_parts)).reshape(4, places.members, -1, D)
    mix_offers = [
        lax.dynamic_index_in_dim(mix_split, (places.member + j) % places.members, 1, False)
        for j in range(places.members)
    ]
    mix_arrived = [places.send(part, "members", j) for j, part in enumerate(mix_offers[1:], 1)]
    wide_grad = summed(*tied(wide_parts, (activations, mix_offers))).astype(BF16)

    wide_low = momentum_rows(wide_mom, wide_grad, wide_blocks)
    wide_known = [wide_low] + to_members(wide_low)
    wide_far = [places.send(wide_low, "chips", k) for k in range(1, places.chips)]
    wide_first = places.send(tied(wide_grad, wide_low), "quads", 1)
    mix_sums = summed(*tied([mix_offers[0]] + mix_arrived, wide_low)).astype(BF16)
    mix_blocks = tied(jnp.stack([mix_sums[i] for i in (2, 0, 1, 3)]), wide_far)
    mix_parts = places.scattered(mix_blocks, "quads")
    mix_grad = summed(*mix_parts).astype(BF16)
    wide_last = [other for part in wide_far for other in to_members(part)]
    wide_known, wide_far = tied((wide_known, wide_far), (mix_parts, wide_last))
    wide_core = jnp.concatenate(wide_known + wide_far, axis=0)
    wide_every = [wide_core, places.send(wide_core, "core", 1)] + wide_last
    wide_every += [places.send(part, "core", 1) for part in wide_last]

    mix_low = momentum_rows(mix_mom, mix_grad, wide_blocks)
    rows, own = wide_grad.shape[0], mix_grad.shape[0]
    mix_others = to_members(jnp.concatenate([mix_low, mix_grad], axis=0))
    mix_known = jnp.concatenate([mix_low] + [part[:own] for part in mix_others], axis=0)
    mix_every = lax.all_gather(mix_known, "batch", axis=0, tiled=True)

    wide_all, mix_all = Blocks(places, rows), Blocks(places, own)
    wide_all.add(wide_grad, (0, 0, 0))
    wide_all.add(wide_first, (0, 1, 0))
    mix_all.add(mix_grad, (0, 0, 0))
    for j, part in enumerate(mix_others, 1):
        mix_all.add(part, (own, 0, j))
    both = jnp.concatenate([wide_grad, mix_grad], axis=0)
    mix_first = places.send(tied(mix_grad, mix_low), "quads", 1)
    both = tied(both, (mix_low, mix_first))
    second, third = (places.send(both, "quads", k) for k in (2, 3))
    early = jnp.concatenate(tied([wide_grad, wide_first], mix_known), axis=0)
    early_arrived = to_members(early)
    for j, part in enumerate(early_arrived, 1):
        wide_all.add(part, (0, 0, j), (rows, 1, j))

    wide_rows, wide_rest = newton_rows(tied(wide_every, (early, mix_known)), wide_core[: rows * places.members], rows)
    wide_x, mix_x = Blocks(places, rows), Blocks(places, own)
    wide_x.add(wide_rows, (0, 0, 0))
    wide_x.add(wide_rest, *[((j - 1) * rows, 0, j) for j in range(1, places.members)])
    x_sent = tied(wide_rows, mix_every)
    x_parts = [places.send(x_sent, "quads", k) for k in (1, 2)]
    mix_rows, mix_rest = newton_rows([tied(mix_every, (wide_rows, early_arrived))], mix_known, own)
    later = jnp.concatenate(tied([second, third, mix_first], mix_rows), axis=0)
    wide_all.add(second, (0, 2, 0))
    wide_all.add(third, (0, 3, 0))
    mix_all.add(mix_first, (0, 1, 0))
    mix_all.add(second, (rows, 2, 0))
    mix_all.add(third, (rows, 3, 0))
    for j, part in enumerate(to_members(later), 1):
        step = rows + own
        wide_all.add(part, (0, 2, j), (step, 3, j))
        mix_all.add(part, (2 * step, 1, j), (rows, 2, j), (step + rows, 3, j))
    x_parts.append(places.send(tied(x_sent, mix_rows), "quads", 3))
    for k, part in enumerate(x_parts, 1):
        wide_x.add(part, (0, k, 0))
    x_pair = jnp.concatenate(tied(x_parts[:2], mix_rows), axis=0)
    x_arrived = to_members(x_pair)
    for j, part in enumerate(x_arrived, 1):
        wide_x.add(part, (0, 1, j), (rows, 2, j))
    mix_x.add(mix_rows, (0, 0, 0))
    mix_x.add(mix_rest, *[((j - 1) * own, 0, j) for j in range(1, places.members)])
    mix_sent = tied(mix_rows, (x_pair, x_parts[2]))
    mix_parts = [places.send(mix_sent, "quads", k) for k in (1, 2, 3)]
    x_last = to_members(x_parts[2])
    for j, part in enumerate(x_last, 1):
        wide_x.add(part, (0, 3, j))
    for k, part in enumerate(mix_parts, 1):
        mix_x.add(part, (0, k, 0))
    for j, part in enumerate(to_members(jnp.concatenate(tied(mix_parts, x_last), axis=0)), 1):
        mix_x.add(part, *[((k - 1) * own, k, j) for k in (1, 2, 3)])

    hidden_rows, width_rows = w_down.shape[0] // places.members, w_out.shape[0] // places.members
    wide_groups = [(0, None, hidden_rows), (1, 0, hidden_rows), (1, 1, hidden_rows), (2, None, width_rows)]
    mix_groups = [(0, i, width_rows) for i in range(4)]
    ones = [1.0] * 4
    mom_down, mom_in, mom_out = wide_all.finished(
        (m_down, m_in, m_out), wide_groups, (MOMENTUM, ones), late=x_last
    )
    (mom_mix,) = mix_all.finished((m_mix,), mix_groups, (MOMENTUM, ones), late=x_last)
    factor = math.sqrt(FF / D)
    steps = [-STEP_RATE, -STEP_RATE * factor, -STEP_RATE * factor, -STEP_RATE]
    new_down, new_in, new_out, copy_down, copy_in, copy_out = wide_x.finished(
        (w_down, w_in, w_out), wide_groups, (1.0, steps), True, late=(mom_down, mom_in, mom_out, mom_mix)
    )
    new_mix, copy_mix = mix_x.finished((w_mix,), mix_groups, (1.0, [-STEP_RATE] * 4), True, late=new_in)
    return (
        activations.reshape(tokens.shape),
        input_grad,
        mom_mix,
        mom_out,
        mom_in,
        mom_down,
        new_mix,
        new_out,
        new_in,
        new_down,
        copy_mix,
        copy_out,
        copy_in,
        copy_down,
    )


def solution(mesh):
    batch_rows = P(None, "batch", None)
    flat_rows = P("batch", None)
    block = P("batch", "seq", None)
    four = (batch_rows, flat_rows, batch_rows, flat_rows)
    in_specs = (block, block, P(None, "seq")) + four + four
    out_specs = (block, block) + four + four + four
    return jax.shard_map(shards, mesh=mesh, in_specs=in_specs, out_specs=out_specs, check_vma=False)
```

```python
import math

import jax
import jax.numpy as jnp
from jax import lax
from jax.experimental import pallas as pl
from jax.experimental.pallas import tpu as pltpu
from jax.sharding import PartitionSpec as P

D = 1024
HEAD_COUNT = 16
HEAD_DIM = 64
FF = 2816
ITERS = 5
PAIRS = HEAD_COUNT // 2
LANES = 2 * HEAD_DIM
TILE = 256
HEADS_PER_TILE = TILE // HEAD_DIM
PAIRS_PER_TILE = TILE // LANES
QUADS = 4

EPSILON = 1e-06
NORM_FLOOR = 1e-07
COEFF_A = 3.4445
COEFF_B = -4.775
COEFF_C = 2.0315
MOMENTUM = 0.5
STEP_RATE = 0.8

F32 = jnp.float32
BF16 = jnp.bfloat16
MIB = 1024 * 1024


def dot_nn(left, right):
    return lax.dot_general(left, right, (((1,), (0,)), ((), ())), preferred_element_type=F32)


def dot_nt(left, right):
    return lax.dot_general(left, right, (((1,), (1,)), ((), ())), preferred_element_type=F32)


def dot_tn(left, right):
    return lax.dot_general(left, right, (((0,), (0,)), ((), ())), preferred_element_type=F32)


def silu_grad(inputs):
    sigma = jax.nn.sigmoid(inputs)
    return sigma * (1.0 + inputs * (1.0 - sigma))


def inverse_rms(inputs):
    return lax.rsqrt(jnp.mean(inputs * inputs, axis=-1, keepdims=True) + EPSILON)


def normalize_back(inputs, grad):
    factor = inverse_rms(inputs)
    normed = inputs * factor
    return factor * (grad - normed * jnp.mean(grad * normed, axis=-1, keepdims=True))


def first_half(shape):
    return lax.broadcasted_iota(jnp.int32, shape, len(shape) - 1) < HEAD_DIM


def head_parts(pair):
    low = first_half(pair.shape)
    zero = jnp.zeros_like(pair)
    return (jnp.where(low, pair, zero), jnp.where(low, zero, pair))


def compact(full):
    return jnp.where(first_half((HEAD_DIM, LANES)), full[:HEAD_DIM], full[HEAD_DIM:])


def expand(state):
    return jnp.concatenate(head_parts(state), axis=0)


def params(limit=56):
    return pltpu.CompilerParams(vmem_limit_bytes=limit * MIB)


def cost(flops, nbytes, share=0.1):
    return pl.CostEstimate(flops=int(flops / share), bytes_accessed=int(nbytes / share), transcendentals=0)


def whole(shape):
    return pl.BlockSpec(shape, lambda i: (0,) * len(shape))


def cols(rows, width=TILE):
    return pl.BlockSpec((rows, width), lambda i: (0, i))


def rows_of(rows, width=D):
    return pl.BlockSpec((rows, width), lambda i: (i, 0))


def exact(left, right, dims):
    return lax.dot_general(
        left, right, (dims, ((), ())), preferred_element_type=F32, precision=lax.Precision.HIGHEST
    )


def decay_kernel(log_ref, last_ref, cum_ref, lead_ref, trail_ref, mask_ref, mask_t_ref):
    logs = log_ref[...]
    length = logs.shape[1]
    row = lax.broadcasted_iota(jnp.int32, (length, length), 0)
    col = lax.broadcasted_iota(jnp.int32, (length, length), 1)
    cum = exact(logs, (row <= col).astype(F32), ((1,), (0,)))
    cum_ref[...] = cum
    last = cum[:, length - 1 :]
    last_ref[...] = last
    lane = lax.broadcasted_iota(jnp.int32, (HEAD_COUNT, D), 1) // HEAD_DIM
    spread = (lane == lax.broadcasted_iota(jnp.int32, (HEAD_COUNT, D), 0)).astype(F32)
    lead_ref[...] = jnp.exp(exact(cum, spread, ((0,), (0,))))
    trail_ref[...] = jnp.exp(exact(last - cum, spread, ((0,), (0,))))
    upright = cum.T
    for h in range(HEAD_COUNT):
        span = upright[:, h : h + 1] - cum[h : h + 1, :]
        mask_ref[h] = jnp.where(row >= col, jnp.exp(jnp.minimum(span, 0.0)), 0.0)
        mask_t_ref[h] = jnp.where(col >= row, jnp.exp(jnp.minimum(-span, 0.0)), 0.0)


def factor_kernel(members, place_ref, logs_ref, out_ref):
    logs = logs_ref[...]
    count = logs.shape[0]
    quad, member = place_ref[0], place_ref[1]
    here = quad * members + member
    start, end = quad * members, quad * members + members - 1
    row = lax.broadcasted_iota(jnp.int32, (count, count), 0)
    col = lax.broadcasted_iota(jnp.int32, (count, count), 1)
    before = exact((col < row).astype(F32), logs, ((1,), (0,)))
    through = before + logs
    at_row = lax.broadcasted_iota(jnp.int32, (count, HEAD_COUNT), 0)

    def at(sums, i):
        return jnp.sum(jnp.where(at_row == i, sums, 0.0), axis=0, keepdims=True)

    def factor(log, valid=True):
        return jnp.where(valid, jnp.exp(jnp.minimum(log, 0.0)), 0.0)

    rows = []
    for backward in (False, True):
        for k in range(1, QUADS):
            if backward:
                rows.append(factor(at(before, here + k * members) - at(through, end), quad + k < QUADS))
            else:
                rows.append(factor(at(before, start) - at(through, here - k * members), quad - k >= 0))
        spots = [lax.rem(member + k, members) for k in range(members)]
        for spot in spots:
            there = start + spot
            rows.append(factor(at(through, end) - at(through, there) if backward else at(before, there) - at(before, start)))
        for spot in spots:
            there = start + spot
            if backward:
                rows.append(factor(at(before, here) - at(through, there), spot < member))
            else:
                rows.append(factor(at(before, there) - at(through, here), spot > member))
    lane = lax.broadcasted_iota(jnp.int32, (HEAD_COUNT, D), 1) // HEAD_DIM
    spread = (lane == lax.broadcasted_iota(jnp.int32, (HEAD_COUNT, D), 0)).astype(F32)
    out_ref[...] = exact(jnp.concatenate(rows, axis=0), spread, ((1,), (0,)))


def kv_kernel(seqs, x_ref, w_ref, trail_ref, normed_ref, pk_ref, k_ref, v_ref, state_ref):
    @pl.when(pl.program_id(0) == 0)
    def _():
        inputs = x_ref[...].astype(F32)
        normed_ref[...] = (inputs * inverse_rms(inputs)).astype(BF16)

    normed = normed_ref[...]
    pre_k = dot_nn(normed, w_ref[0])
    keys = pre_k * jax.nn.sigmoid(pre_k)
    values = dot_nn(normed, w_ref[1]).astype(BF16)
    pk_ref[...] = pre_k.astype(BF16)
    k_ref[...] = keys.astype(BF16)
    v_ref[...] = values
    trail = trail_ref[...]
    length = trail.shape[0]
    for b in range(seqs):
        at = slice(b * length, (b + 1) * length)
        scaled = (keys[at] * trail).astype(BF16)
        for p in range(PAIRS_PER_TILE):
            lanes = slice(p * LANES, (p + 1) * LANES)
            state_ref[b, p] = compact(dot_tn(scaled[:, lanes], values[at, lanes])).astype(BF16)


def q_kernel(seqs, normed_ref, w_ref, k_ref, v_ref, mask_ref, pq_ref, q_ref, pg_ref, o_ref):
    normed = normed_ref[...]
    pre_q = dot_nn(normed, w_ref[0])
    pq_ref[...] = pre_q.astype(BF16)
    q_ref[...] = (pre_q * jax.nn.sigmoid(pre_q)).astype(BF16)
    pg_ref[...] = dot_nn(normed, w_ref[1]).astype(BF16)
    length = mask_ref.shape[1]
    for b in range(seqs):
        at = slice(b * length, (b + 1) * length)
        for p in range(PAIRS_PER_TILE):
            lanes = slice(p * LANES, (p + 1) * LANES)
            q_parts = head_parts(q_ref[at, lanes])
            v_parts = head_parts(v_ref[at, lanes])
            keys = k_ref[at, lanes]
            total = jnp.zeros((length, LANES), F32)
            for h in range(2):
                scores = dot_nt(q_parts[h], keys) * mask_ref[2 * p + h]
                total = total + dot_nn(scores.astype(BF16), v_parts[h])
            o_ref[at, lanes] = total


def mid_kernel(o_ref, q_ref, state_ref, lead_ref, pg_ref, x_ref, wo_ref, att_ref, hid_ref, mid_ref, nf_ref):
    scaled = (q_ref[...].astype(F32) * lead_ref[...]).astype(BF16)
    for p in range(PAIRS):
        lanes = slice(p * LANES, (p + 1) * LANES)
        att_ref[:, lanes] = o_ref[:, lanes] + dot_nn(scaled[:, lanes], expand(state_ref[0, p]))
    attended = att_ref[...]
    gate_in = pg_ref[...].astype(F32)
    hidden = (attended * inverse_rms(attended) * gate_in * jax.nn.sigmoid(gate_in)).astype(BF16)
    hid_ref[...] = hidden
    middle = x_ref[...].astype(F32) + dot_nn(hidden, wo_ref[...])
    mid_ref[...] = middle
    nf_ref[...] = (middle * inverse_rms(middle)).astype(BF16)


def ffn_kernel(carry, last, more, cut, place_ref, x_refs, out_refs, buffers, sems):
    nf_buf, cot_buf, w_in_buf, w_down_buf, out_buf, dn_buf, prod_buf, first_buf, second_buf, grad_buf = buffers[:10]
    rows = grad_buf.shape[1]
    if place_ref is None:
        targets = [nf_buf, w_in_buf, cot_buf, w_down_buf]
    else:
        half = rows // 2
        here = pl.ds(pl.multiple_of(place_ref[0] * half, half), half)
        there = pl.ds(pl.multiple_of((1 - place_ref[0]) * half, half), half)
        targets = [nf_buf, w_in_buf.at[:, here], w_in_buf.at[:, there], cot_buf, w_down_buf.at[here], w_down_buf.at[there]]
    needed = len(targets)
    targets = targets + [out_buf, dn_buf][:carry] + ([grad_buf] if more else [])
    loads = [
        pltpu.make_async_copy(source, target, sems.at[i]) for i, (source, target) in enumerate(zip(x_refs, targets))
    ]
    for load in loads:
        load.start()
    sum_bufs = buffers[10:] if last else (out_buf, dn_buf)
    out_copies = [pltpu.make_async_copy(buf, ref, sems.at[9 + i]) for i, (buf, ref) in enumerate(zip(sum_bufs, out_refs))]
    pieces = [pl.ds(0, cut), pl.ds(cut, rows - cut)] if cut else [pl.ds(0, rows)]
    grad_copies = [
        [
            pltpu.make_async_copy(grad_buf.at[i, piece], out_refs[2 + j].at[i], sems.at[11 + 2 * i + j])
            for j, piece in enumerate(pieces)
        ]
        for i in range(3)
    ]
    count = nf_buf.shape[0]
    first_half = 2 if place_ref is None else 3
    step = min(TILE, count)
    for at in [slice(t, t + step) for t in range(0, count, step)]:
        if at.start == 0:
            for load in loads[:first_half]:
                load.wait()
        normed = nf_buf[at, :]
        first = dot_nt(w_in_buf[0], normed)
        second = dot_nt(w_in_buf[1], normed)
        if at.start == 0:
            for load in loads[first_half:needed]:
                load.wait()
        cot = cot_buf[at, :]
        d_product = dot_nt(w_down_buf[...], cot)
        product = (first * second).astype(BF16)
        d_first = (d_product * second).astype(BF16)
        d_second = (d_product * first).astype(BF16)
        prod_buf[:, at] = product
        first_buf[:, at] = d_first
        second_buf[:, at] = d_second
        out = dot_tn(product, w_down_buf[...])
        d_normed = dot_tn(d_first, w_in_buf[0]) + dot_tn(d_second, w_in_buf[1])
        if at.start == 0:
            for load in loads[needed:]:
                load.wait()
        if carry > 0:
            out = out_buf[at, :] + out
        if carry > 1:
            d_normed = dn_buf[at, :] + d_normed
        sum_bufs[0][at, :] = out.astype(sum_bufs[0].dtype)
        sum_bufs[1][at, :] = d_normed.astype(sum_bufs[1].dtype)
    for copy in out_copies:
        copy.start()
    for i, (left, right) in enumerate(((first_buf, nf_buf), (second_buf, nf_buf), (prod_buf, cot_buf))):
        for at in [slice(c, c + TILE) for c in range(0, D, TILE)]:
            grad = dot_nn(left[...], right[:, at])
            if more:
                grad = grad + grad_buf[i, :, at].astype(F32)
            grad_buf[i, :, at] = grad.astype(BF16)
        for copy in grad_copies[i]:
            copy.start()
    for copy in out_copies + [copy for copies in grad_copies for copy in copies]:
        copy.wait()


def ffn(normed, cot, weights, sums=(), last=False, grads=None, cut=0, place=None):
    w_in, w_down = ((w,) if place is None else w for w in weights)
    count, rows = normed.shape[0], sum(part.shape[0] for part in w_down)
    away = pl.BlockSpec(memory_space=pl.ANY)
    kind = BF16 if last else F32
    ins = (normed, *w_in, cot, *w_down, *sums) + (() if grads is None else (grads,))
    places = () if place is None else (place,)
    n_in = len(ins)
    parts = [cut, rows - cut] if cut else [rows]
    n_out = 2 + len(parts)
    has_grads = grads is not None

    def body(*refs):
        place_ref = refs[0] if places else None
        refs = refs[len(places) :]
        outs, buffers = refs[n_in : n_in + n_out], refs[n_in + n_out : -1]
        ffn_kernel(len(sums), last, has_grads, cut, place_ref, refs[:n_in], outs, buffers, refs[-1])

    tokens_by = pltpu.VMEM((count, D), BF16)
    units_by = pltpu.VMEM((rows, count), BF16)
    out, d_normed, *grads = pl.pallas_call(
        body,
        in_specs=[pl.BlockSpec(memory_space=pltpu.SMEM)] * len(places) + [away] * n_in,
        out_specs=[away] * n_out,
        out_shape=[jax.ShapeDtypeStruct((count, D), kind)] * 2
        + [jax.ShapeDtypeStruct((3, part, D), BF16) for part in parts],
        scratch_shapes=[tokens_by, tokens_by, pltpu.VMEM((2, rows, D), BF16), pltpu.VMEM((rows, D), BF16)]
        + [pltpu.VMEM((count, D), F32)] * 2
        + [units_by] * 3
        + [pltpu.VMEM((3, rows, D), BF16)]
        + ([tokens_by] * 2 if last else [])
        + [pltpu.SemaphoreType.DMA((17,))],
        compiler_params=params(60),
        cost_estimate=cost(16 * count * D * rows, 12 * rows * D + 12 * count * D),
        name="ffn",
    )(*places, *ins)
    return (out, d_normed), grads


def gate_back_kernel(
    dn_ref, dn_mate_ref, mid_ref, cot_ref, wo_ref, att_ref, pg_ref, q_ref, lead_ref, *out_refs
):
    dmid_ref, datt_ref, dgate_ref, state_ref = out_refs
    d_normed_ffn = dn_ref[...] + dn_mate_ref[...].astype(F32)
    d_middle = cot_ref[...].astype(F32) + normalize_back(mid_ref[...], d_normed_ffn)
    d_middle = d_middle.astype(BF16)
    dmid_ref[...] = d_middle
    d_hidden = dot_nt(d_middle, wo_ref[...])
    attended = att_ref[...]
    factor = inverse_rms(attended)
    out_norm = attended * factor
    gate_in = pg_ref[...].astype(F32)
    sigma = jax.nn.sigmoid(gate_in)
    dgate_ref[...] = (d_hidden * out_norm * sigma * (1.0 + gate_in * (1.0 - sigma))).astype(BF16)
    grad = d_hidden * gate_in * sigma
    d_att = factor * (grad - out_norm * jnp.mean(grad * out_norm, axis=-1, keepdims=True))
    d_att = d_att.astype(BF16)
    datt_ref[...] = d_att
    scaled = (q_ref[...].astype(F32) * lead_ref[...]).astype(BF16)
    for p in range(PAIRS):
        lanes = slice(p * LANES, (p + 1) * LANES)
        state_ref[0, p] = compact(dot_tn(scaled[:, lanes], d_att[:, lanes])).astype(BF16)


def early_grads_kernel(hid_ref, nf_ref, dmid_ref, dgate_ref, out_grad_ref, gate_grad_ref):
    out_grad_ref[0] = dot_tn(hid_ref[...], dmid_ref[...]).astype(BF16)
    gate_grad_ref[0] = dot_tn(nf_ref[...], dgate_ref[...]).astype(BF16)


def att_back_kernel(
    seqs, q_ref, k_ref, v_ref, da_ref, pq_ref, mask_ref, mask_t_ref, state_ref, lead_ref, nf_ref, *out_refs
):
    dq_ref, dk_ref, dv_ref, grad_ref = out_refs[1:]
    lead = lead_ref[...]
    length = lead.shape[0]
    for b in range(seqs):
        at = slice(b * length, (b + 1) * length)
        for p in range(PAIRS_PER_TILE):
            lanes = slice(p * LANES, (p + 1) * LANES)
            queries, keys, values, d_att = (r[at, lanes] for r in (q_ref, k_ref, v_ref, da_ref))
            q_parts, k_parts, v_parts, d_parts = (head_parts(a) for a in (queries, keys, values, d_att))
            d_q = dot_nt((d_att.astype(F32) * lead[:, lanes]).astype(BF16), expand(state_ref[b, p]))
            d_k = jnp.zeros((length, LANES), F32)
            d_v = jnp.zeros((length, LANES), F32)
            for h in range(2):
                mask, mask_t = mask_ref[2 * p + h], mask_t_ref[2 * p + h]
                d_scores = (dot_nt(d_parts[h], values) * mask).astype(BF16)
                d_scores_t = (dot_nt(v_parts[h], d_att) * mask_t).astype(BF16)
                scores_t = (dot_nt(k_parts[h], queries) * mask_t).astype(BF16)
                d_q = d_q + dot_nn(d_scores, k_parts[h])
                d_k = d_k + dot_nn(d_scores_t, q_parts[h])
                d_v = d_v + dot_nn(scores_t, d_parts[h])
            dq_ref[at, lanes] = (d_q * silu_grad(pq_ref[at, lanes].astype(F32))).astype(BF16)
            dk_ref[at, lanes] = d_k
            dv_ref[at, lanes] = d_v
    grad_ref[0] = dot_tn(nf_ref[...], dq_ref[...]).astype(BF16)


def state_back_kernel(
    seqs, k_ref, v_ref, pk_ref, dk_in_ref, dv_in_ref, state_ref, trail_ref, nf_ref, _, dkv_ref, grad_ref
):
    trail = trail_ref[...]
    length = trail.shape[0]
    for b in range(seqs):
        at = slice(b * length, (b + 1) * length)
        k_scaled = (k_ref[at, :].astype(F32) * trail).astype(BF16)
        v_scaled = (v_ref[at, :].astype(F32) * trail).astype(BF16)
        for p in range(PAIRS_PER_TILE):
            lanes = slice(p * LANES, (p + 1) * LANES)
            state = expand(state_ref[b, p])
            d_k = dk_in_ref[at, lanes] + dot_nt(v_scaled[:, lanes], state)
            d_v = dv_in_ref[at, lanes] + dot_nn(k_scaled[:, lanes], state)
            dkv_ref[0, at, lanes] = (d_k * silu_grad(pk_ref[at, lanes].astype(F32))).astype(BF16)
            dkv_ref[1, at, lanes] = d_v.astype(BF16)
    for i in range(2):
        grad_ref[i] = dot_tn(nf_ref[...], dkv_ref[i]).astype(BF16)


def dots_back_kernel(dq_ref, dg_ref, w_ref, out_ref):
    out_ref[...] = dot_nt(dq_ref[...], w_ref[0]) + dot_nt(dg_ref[...], w_ref[1])


def input_back_kernel(dkv_ref, w_ref, part_ref, x_ref, dmid_ref, out_ref):
    d_normed = part_ref[...] + dot_nt(dkv_ref[0], w_ref[0]) + dot_nt(dkv_ref[1], w_ref[1])
    d_tokens = dmid_ref[...].astype(F32) + normalize_back(x_ref[...].astype(F32), d_normed)
    out_ref[...] = d_tokens.astype(BF16)


def newton_kernel(parts, *refs):
    b_refs, (row_ref, out_ref, rest_ref, g_ref, gb_ref, nb_ref, h_ref, hb_ref, x_ref) = refs[:parts], refs[parts:]
    tiles = [slice(i * TILE, (i + 1) * TILE) for i in range(D // TILE)]

    def right_of(at):
        return slice(at.start, D)

    def mirrored(target, at, part):
        low = part.astype(BF16)
        target[at, right_of(at)] = low
        for other in tiles:
            if other.start > at.start:
                target[other, at] = low[:, other.start - at.start : other.stop - at.start].T

    trace = jnp.zeros((1, 1), F32)
    for at in tiles:
        part = sum(dot_tn(b_ref[:, at], b_ref[:, right_of(at)]) for b_ref in b_refs)
        g_ref[at, right_of(at)] = part
        on_row = lax.broadcasted_iota(jnp.int32, (TILE, TILE), 0)
        on_col = lax.broadcasted_iota(jnp.int32, (TILE, TILE), 1)
        trace = trace + jnp.sum(jnp.where(on_row == on_col, part[:, :TILE], 0.0), keepdims=True)
    inverse = 1.0 / (jnp.sqrt(trace) + NORM_FLOOR)
    x_ref[...] = row_ref[...].astype(F32) * inverse
    scale = inverse * inverse
    for at in tiles:
        gram = g_ref[at, right_of(at)] * scale
        g_ref[at, right_of(at)] = gram
        mirrored(gb_ref, at, gram)

    def polynomial():
        for at in tiles:
            square = dot_nn(gb_ref[at, :], gb_ref[:, right_of(at)])
            mirrored(nb_ref, at, COEFF_B * g_ref[at, right_of(at)] + COEFF_C * square)
        state = x_ref[...]
        x_ref[...] = COEFF_A * state + dot_nn(state.astype(BF16), nb_ref[...])

    @pl.loop(0, ITERS - 1)
    def _(turn):
        polynomial()
        for at in tiles:
            half = COEFF_A * g_ref[at, right_of(at)] + dot_nn(gb_ref[at, :], nb_ref[:, right_of(at)])
            h_ref[at, right_of(at)] = half
            mirrored(hb_ref, at, half)
        for at in tiles:
            gram = COEFF_A * h_ref[at, right_of(at)] + dot_nn(nb_ref[at, :], hb_ref[:, right_of(at)])
            g_ref[at, right_of(at)] = gram
            mirrored(gb_ref, at, gram)

    polynomial()
    own = out_ref.shape[0]
    out_ref[...] = x_ref[:own, :].astype(BF16)
    rest_ref[...] = x_ref[own:, :].astype(BF16)


def newton_rows(every, mine, first):
    rows, own = sum(part.shape[0] for part in every), mine.shape[0]
    return pl.pallas_call(
        lambda *refs: newton_kernel(len(every), *refs),
        out_shape=[jax.ShapeDtypeStruct((first, D), BF16), jax.ShapeDtypeStruct((own - first, D), BF16)],
        grid=(1,),
        in_specs=[whole(part.shape) for part in every] + [whole((own, D))],
        out_specs=[whole((first, D)), whole((own - first, D))],
        scratch_shapes=[
            pltpu.VMEM((D, D), F32),
            pltpu.VMEM((D, D), BF16),
            pltpu.VMEM((D, D), BF16),
            pltpu.VMEM((D, D), F32),
            pltpu.VMEM((D, D), BF16),
            pltpu.VMEM((own, D), F32),
        ],
        compiler_params=params(),
        cost_estimate=cost(2 * D * D * (13 * D + rows + 5 * own), 2 * D * (rows + 2 * own)),
        name="newton",
    )(*every, mine)


class Places:
    def __init__(self):
        self.members = lax.axis_size("seq") // QUADS
        self.chips = lax.axis_size("batch") // 2
        at = lax.axis_index("seq").astype(jnp.uint32)
        self.quad, self.member = at // self.members, at % self.members
        at = lax.axis_index("batch").astype(jnp.uint32)
        self.chip, self.core = at // 2, at % 2

    def level(self, name):
        return {
            "quads": (QUADS, self.quad),
            "members": (self.members, self.member),
            "chips": (self.chips, self.chip),
            "core": (2, self.core),
        }[name]

    def send(self, value, name, k, wrap=True):
        pairs = []
        if name in ("quads", "members"):
            for q in range(QUADS):
                for m in range(self.members):
                    if name == "members":
                        pairs.append((q * self.members + m, q * self.members + (m + k) % self.members))
                    elif wrap or 0 <= q + k < QUADS:
                        pairs.append((q * self.members + m, (q + k) % QUADS * self.members + m))
            return lax.ppermute(value, "seq", pairs)
        for x in range(self.chips):
            for c in range(2):
                to = 2 * x + (c + k) % 2 if name == "core" else (x + k) % self.chips * 2 + c
                pairs.append((2 * x + c, to))
        return lax.ppermute(value, "batch", pairs)

    def pair(self, value):
        pairs = []
        for q in range(QUADS):
            for m in range(self.members):
                pairs.append((q * self.members + m, (q ^ 1) * self.members + m))
        return lax.ppermute(value, "seq", pairs)

    def scattered(self, blocks, name, axis=0):
        count, mine = self.level(name)

        def block(j):
            return lax.dynamic_index_in_dim(blocks, j, axis, False)

        return [block(mine)] + [self.send(block((mine + k) % count), name, k) for k in range(1, count)]

    def scatter(self, blocks, name, axis=0):
        return summed(*self.scattered(blocks, name, axis)).astype(BF16)

    def gather(self, block, name, axis=0):
        count, mine = self.level(name)
        shape = block.shape[:axis] + (count,) + block.shape[axis:]
        result = jnp.zeros(shape, block.dtype)
        result = lax.dynamic_update_index_in_dim(result, block, mine, axis)
        for k in range(1, count):
            part = self.send(block, name, k)
            result = lax.dynamic_update_index_in_dim(result, part, (mine + (count - k)) % count, axis)
        return result

    def far_rows(self, own, after, pair_after, use_after):
        n, rows, _ = own.shape
        split = own.reshape(n, 2, rows // 2, D)
        mine = tied(lax.dynamic_index_in_dim(split, self.quad % 2, 1, False), after)
        far = []
        for k in range(1, self.chips):
            part = tied(self.send(mine, "chips", k), pair_after)
            far.append(tied((part, self.pair(part)), use_after))
        return far


def tied(value, *others):
    return lax.optimization_barrier((value, others))[0]


class Carried:
    def __init__(self, places, local, factors, backward):
        self.places = places
        factors = factors.reshape(-1, PAIRS, 1, LANES)
        self.quad_factors = factors[: QUADS - 1]
        self.spot_factors = factors[QUADS - 1 : QUADS - 1 + places.members]
        self.local_factors = factors[QUADS - 1 + places.members :]
        self.local = local
        sign = -1 if backward else 1
        self.arrived = [places.send(self.local, "quads", sign * k, wrap=False) for k in range(1, QUADS)]

    def finish(self, after=()):
        outer = sum(part.astype(F32) * self.quad_factors[k] for k, part in enumerate(self.arrived))
        local = self.local.astype(F32)
        own = self.spot_factors[0] * outer
        self.sent = [
            tied((self.spot_factors[k] * outer + self.local_factors[k] * local).astype(BF16), after)
            for k in range(1, self.places.members)
        ]
        parts = [self.places.send(part, "members", k) for k, part in enumerate(self.sent, 1)]
        return summed(own, *parts).astype(BF16)


def padded(block, rows):
    return jnp.pad(block, ((0, rows - block.shape[0]), (0, 0)))


def summed(*parts):
    total = parts[0].astype(F32)
    for part in parts[1:]:
        total = total + part.astype(F32)
    return total


class WideSum:
    def __init__(self, places, rows):
        self.places = places
        self.shape = (3, places.members, rows // places.members, D)

    def ordered(self, weights):
        places = self.places
        split = weights.reshape(weights.shape[0], places.members, -1, D)
        parts = [
            lax.dynamic_index_in_dim(split, (places.member + k) % places.members, 1, False)
            for k in range(places.members)
        ]
        return jnp.concatenate(parts, axis=1).astype(BF16)

    def cut(self):
        own = self.shape[2]
        return own if own % 16 == 0 else 0

    def parts(self, grads):
        if len(grads) == 1:
            split = grads[0].reshape(self.shape)
            return split[:, 0], [split[:, k] for k in range(1, self.places.members)]
        split = grads[1].reshape((3, -1) + self.shape[2:])
        if self.places.members == 2:
            return grads[0], [grads[1]]
        return grads[0], [split[:, k] for k in range(self.places.members - 1)]

    def exchange(self, offers):
        return [self.places.send(offer, "members", k + 1) for k, offer in enumerate(offers)]


def place_kernel(members, rows, sources, place_ref, *refs):
    sources_refs, out_ref, sems = refs[:-2], refs[-2], refs[-1]
    quad, member = place_ref[0], place_ref[1]
    copies = []
    for i, (ref, start, k, j) in enumerate(sources):
        q, m = lax.rem(quad + (QUADS - k), QUADS), lax.rem(member + (members - j), members)
        block = sources_refs[ref].at[pl.ds(start, rows)]
        copies.append(pltpu.make_async_copy(block, out_ref.at[q, m], sems.at[i]))
    for copy in copies:
        copy.start()
    for copy in copies:
        copy.wait()


def finish_kernel(members, sources, groups, scales, copies, place_ref, *refs):
    count = len({array for array, _, _ in groups})
    n_blocks = len({ref for ref, _, _, _ in sources})
    block_refs, refs = refs[:n_blocks], refs[n_blocks:]
    base_refs, refs = refs[:count], refs[count:]
    out_refs, refs = refs[:count], refs[count:]
    if copies:
        low_refs, refs = refs[:count], refs[count:]
        block_buf, base_buf, low_buf, sems = refs
    else:
        block_buf, base_buf, sems = refs
    quad, member = place_ref[0], place_ref[1]
    rows = block_buf.shape[2]
    loads = []
    for i, (ref, start, k, j) in enumerate(sources):
        q, m = lax.rem(quad + (QUADS - k), QUADS), lax.rem(member + (members - j), members)
        block = block_refs[ref].at[pl.ds(start, rows)]
        loads.append(pltpu.make_async_copy(block, block_buf.at[q, m], sems.at[0, i]))

    def whole_of(ref, q):
        array, at, _ = groups[q]
        return ref[array] if at is None else ref[array].at[at]

    def used(buf, q):
        return buf.at[q, pl.ds(0, members * groups[q][2])]

    bases = [pltpu.make_async_copy(whole_of(base_refs, q), used(base_buf, q), sems.at[1, q]) for q in range(QUADS)]
    for copy in loads + bases:
        copy.start()
    for copy in loads:
        copy.wait()
    stores = []
    for q in range(QUADS):
        bases[q].wait()
        own = groups[q][2]
        for m in range(members):
            at = slice(m * own, (m + 1) * own)
            value = scales[0] * base_buf[q, at] + scales[1][q] * block_buf[q, m, :own].astype(F32)
            base_buf[q, at] = value
            if copies:
                low_buf[q, at] = value.astype(BF16)
        store = [pltpu.make_async_copy(used(base_buf, q), whole_of(out_refs, q), sems.at[2, q])]
        if copies:
            store.append(pltpu.make_async_copy(used(low_buf, q), whole_of(low_refs, q), sems.at[3, q]))
        for copy in store:
            copy.start()
        stores += store
    for copy in stores:
        copy.wait()


class Blocks:
    def __init__(self, places, rows):
        self.places, self.rows = places, rows
        self.arrays, self.sources = [], []

    def add(self, array, *blocks):
        whole_tiles = all(n % 16 == 0 for n in (self.rows, *(start for start, _, _ in blocks)))
        for start, k, j in blocks:
            self.sources.append((len(self.arrays), start if whole_tiles else 0, k, j))
            if not whole_tiles:
                self.arrays.append(array[start : start + self.rows])
        if whole_tiles:
            self.arrays.append(array)

    def finished(self, arrays, groups, scales, copies=False, late=()):
        places = self.places
        away = pl.BlockSpec(memory_space=pl.ANY)
        outs = [jax.ShapeDtypeStruct(array.shape, F32) for array in arrays]
        lows = [jax.ShapeDtypeStruct(array.shape, BF16) for array in arrays] if copies else []
        if any(own % 16 for _, _, own in groups):
            blocks = self.placed(late)
            parts = [blocks[q, :, :own].reshape(-1, D).astype(F32) * scales[1][q] for q, (_, _, own) in enumerate(groups)]
            results = []
            for i, array in enumerate(arrays):
                mine = [part for part, (at, _, _) in zip(parts, groups) if at == i]
                results.append(scales[0] * array + jnp.stack(mine).reshape(array.shape))
            return results + [result.astype(BF16) for result in results if copies]
        tall = (QUADS, places.members * self.rows, D)
        return pl.pallas_call(
            lambda *refs: finish_kernel(places.members, self.sources, groups, scales, copies, *refs),
            in_specs=[pl.BlockSpec(memory_space=pltpu.SMEM)] + [away] * (len(self.arrays) + len(arrays)),
            out_specs=[away] * (len(outs) + len(lows)),
            out_shape=outs + lows,
            scratch_shapes=[
                pltpu.VMEM((QUADS, places.members, self.rows, D), BF16),
                pltpu.VMEM(tall, F32),
            ]
            + ([pltpu.VMEM(tall, BF16)] if copies else [])
            + [pltpu.SemaphoreType.DMA((4, len(self.sources)))],
            compiler_params=params(),
            name="finish",
        )(jnp.stack([places.quad, places.member]).astype(jnp.int32), *tied(self.arrays, late), *arrays)

    def placed(self, late=()):
        places = self.places
        away = pl.BlockSpec(memory_space=pl.ANY)
        return pl.pallas_call(
            lambda *refs: place_kernel(places.members, self.rows, self.sources, *refs),
            in_specs=[pl.BlockSpec(memory_space=pltpu.SMEM)] + [away] * len(self.arrays),
            out_specs=pl.BlockSpec(memory_space=pltpu.VMEM),
            out_shape=jax.ShapeDtypeStruct((QUADS, places.members, self.rows, D), BF16),
            scratch_shapes=[pltpu.SemaphoreType.DMA((len(self.sources),))],
            compiler_params=params(),
            name="place",
        )(jnp.stack([places.quad, places.member]).astype(jnp.int32), *tied(self.arrays, late))


def own_rows(places, sources, most):
    result = None
    zero = jnp.uint32(0)
    for i, (source, at) in enumerate(sources):
        rows = source.shape[1] // places.members
        part = lax.dynamic_slice(source, (jnp.uint32(at), places.member * rows, zero), (1, rows, D))[0]
        part = padded(part, most)
        result = part if result is None else jnp.where(places.quad == i, part, result)
    return result


def shards(tokens, cotangent, log_decay, w_mix, w_out, w_in, w_down, m_mix, m_out, m_in, m_down):
    places = Places()
    seqs, length, _ = tokens.shape
    count = seqs * length
    state_shape = (seqs, PAIRS, HEAD_DIM, LANES)
    tiles = D // TILE

    cot = cotangent.reshape(count, D)

    def gathered(*rows):
        return lax.all_gather(jnp.stack(rows).astype(BF16), "batch", axis=1, tiled=True)

    full_kv = gathered(w_mix[1], w_mix[2])
    full_qg = gathered(w_mix[0], w_mix[3])
    full_out = gathered(w_out)[0]
    square = jax.ShapeDtypeStruct((HEAD_COUNT, length, length), F32)
    by_lane = jax.ShapeDtypeStruct((length, D), F32)
    last, _, lead, trail, mask, mask_t = pl.pallas_call(
        decay_kernel,
        out_shape=[
            jax.ShapeDtypeStruct((HEAD_COUNT, 1), F32),
            jax.ShapeDtypeStruct((HEAD_COUNT, length), F32),
            by_lane,
            by_lane,
            square,
            square,
        ],
        compiler_params=params(),
        name="decay",
    )(log_decay)
    decays = places.gather(places.gather(last[:, 0], "members"), "quads").reshape(-1, HEAD_COUNT)
    members = places.members
    factors = pl.pallas_call(
        lambda *refs: factor_kernel(members, *refs),
        in_specs=[pl.BlockSpec(memory_space=pltpu.SMEM), pl.BlockSpec(memory_space=pltpu.VMEM)],
        out_shape=jax.ShapeDtypeStruct((2 * (2 * members + QUADS - 1), D), F32),
        compiler_params=params(),
        name="factors",
    )(jnp.stack([places.quad, places.member]).astype(jnp.int32), decays).reshape(2, -1, D)

    x = tokens.reshape(count, D)

    tile_state = pl.BlockSpec((seqs, PAIRS_PER_TILE, HEAD_DIM, LANES), lambda i: (0, i, 0, 0))
    row_state = pl.BlockSpec((1, PAIRS, HEAD_DIM, LANES), lambda i: (i, 0, 0, 0))
    tile_mask = pl.BlockSpec((HEADS_PER_TILE, length, length), lambda i: (i, 0, 0))
    pair_cols = pl.BlockSpec((2, D, TILE), lambda i: (0, 0, i))
    wide = jax.ShapeDtypeStruct((count, D), F32)
    narrow = jax.ShapeDtypeStruct((count, D), BF16)

    normed, pre_k, keys, values, summary = pl.pallas_call(
        lambda *refs: kv_kernel(seqs, *refs),
        grid=(tiles,),
        in_specs=[whole((count, D)), pair_cols, cols(length)],
        out_specs=[whole((count, D)), cols(count), cols(count), cols(count), tile_state],
        out_shape=[narrow, narrow, narrow, narrow, jax.ShapeDtypeStruct(state_shape, BF16)],
        compiler_params=params(),
        cost_estimate=cost(4 * count * D * D, 16 * count * D),
        name="kv",
    )(x, full_kv, trail)
    ahead = Carried(places, summary, factors[0], False)
    incoming = ahead.finish()

    cot_mate = places.send(tied(cot, full_kv), "core", 1)
    wide_sum = WideSum(places, w_down.shape[0])
    w_in_late, w_down_late = tied((w_in, w_down), full_kv)
    in_low, down_low = wide_sum.ordered(w_in_late), wide_sum.ordered(w_down_late[None])[0]

    pre_q, queries, gate_in, inner = pl.pallas_call(
        lambda *refs: q_kernel(seqs, *refs),
        grid=(tiles,),
        in_specs=[whole((count, D)), pair_cols, cols(count), cols(count), tile_mask],
        out_specs=[cols(count)] * 4,
        out_shape=[narrow, narrow, narrow, wide],
        compiler_params=params(),
        cost_estimate=cost(8 * count * D * D, 16 * count * D),
        name="query",
    )(normed, full_qg, keys, values, mask)

    attended, hidden, middle, normed_ffn = pl.pallas_call(
        mid_kernel,
        grid=(seqs,),
        in_specs=[
            rows_of(length),
            rows_of(length),
            row_state,
            whole((length, D)),
            rows_of(length),
            rows_of(length),
            whole((D, D)),
        ],
        out_specs=[rows_of(length)] * 4,
        out_shape=[wide, narrow, wide, narrow],
        compiler_params=params(),
        cost_estimate=cost(2 * count * D * D, 24 * count * D),
        name="middle",
    )(inner, queries, incoming, lead, gate_in, x, full_out)

    nf_mate = places.send(normed_ffn, "core", 1)
    near_weights = (in_low, down_low)
    sums, near_own = ffn(normed_ffn, cot, near_weights, (middle,))
    nf_mate, cot_mate = tied((nf_mate, cot_mate), sums)
    cut = wide_sum.cut()
    mate_sums, near = ffn(nf_mate, cot_mate, near_weights, grads=near_own[0], cut=cut)
    far_down = places.far_rows(down_low[None], full_qg, normed_ffn, mate_sums)
    far_in = places.far_rows(in_low, queries, sums, mate_sums)
    far_weights = [(part, [half[0] for half in down]) for part, down in zip(far_in, far_down)]
    place = (places.quad % 2).astype(jnp.int32).reshape(1)
    near, near_offers = wide_sum.parts(near)
    near_arrived = wide_sum.exchange(near_offers)
    far = []
    for k, weights in enumerate(far_weights):
        mate_sums = tied(mate_sums, near_offers)
        mate_sums, grad = ffn(nf_mate, cot_mate, weights, mate_sums, k == len(far_weights) - 1, place=place)
        far += grad
    out_mate, dn_mate = mate_sums
    dn_mate = places.send(dn_mate, "core", 1)
    for k, weights in enumerate(far_weights):
        sums, far[k] = ffn(normed_ffn, cot, weights, tied(sums, mate_sums), grads=far[k], cut=cut, place=place)
    far = [wide_sum.parts(grads) for grads in far]
    far_arrived = [wide_sum.exchange(offers) for _, offers in far]

    d_middle, d_attended, d_gate, local_grad = pl.pallas_call(
        gate_back_kernel,
        grid=(seqs,),
        in_specs=[
            rows_of(length),
            rows_of(length),
            rows_of(length),
            rows_of(length),
            whole((D, D)),
            rows_of(length),
            rows_of(length),
            rows_of(length),
            whole((length, D)),
        ],
        out_specs=[rows_of(length), rows_of(length), rows_of(length), row_state],
        out_shape=[narrow, narrow, narrow, jax.ShapeDtypeStruct(state_shape, BF16)],
        compiler_params=params(),
        cost_estimate=cost(2 * count * D * D, 16 * count * D),
        name="gate_back",
    )(sums[1], dn_mate, middle, cot, full_out, attended, gate_in, queries, lead)
    behind = Carried(places, local_grad, factors[1], True)
    one_cols = pl.BlockSpec((1, D, TILE), lambda i: (0, 0, i))
    four_grads = jax.ShapeDtypeStruct((4, D, D), BF16)
    out_grad, mix_grads = pl.pallas_call(
        early_grads_kernel,
        grid=(tiles,),
        in_specs=[whole((count, D)), whole((count, D)), cols(count), cols(count)],
        out_specs=[one_cols, pl.BlockSpec((1, D, TILE), lambda i: (3, 0, i))],
        out_shape=[jax.ShapeDtypeStruct((1, D, D), BF16), four_grads],
        compiler_params=params(),
        cost_estimate=cost(4 * count * D * D, 12 * count * D),
        name="early_grads",
    )(hidden, normed, d_middle, d_gate)
    d_attended = tied(d_attended, near_arrived)
    d_query, d_key_part, d_value_part, mix_grads = pl.pallas_call(
        lambda *refs: att_back_kernel(seqs, *refs),
        grid=(tiles,),
        in_specs=[cols(count)] * 5
        + [tile_mask, tile_mask, tile_state, cols(length), whole((count, D)), pl.BlockSpec(memory_space=pl.ANY)],
        out_specs=[cols(count)] * 3 + [pl.BlockSpec((1, D, TILE), lambda i: (2, 0, i))],
        out_shape=[narrow, wide, wide, four_grads],
        input_output_aliases={10: 3},
        compiler_params=params(),
        cost_estimate=cost(8 * count * D * D, 20 * count * D),
        name="attention_back",
    )(queries, keys, values, d_attended, pre_q, mask, mask_t, incoming, lead, normed, mix_grads)

    def scattered(grads):
        return lax.psum_scatter(grads, "batch", scatter_dimension=1, tiled=True)

    def members_sum(grads):
        n, rows, _ = grads.shape
        return places.scatter(grads.reshape(n, places.members, rows // places.members, D), "members", 1)

    sum_out = scattered(out_grad)
    far_sums = [
        tied(summed(own, *arrived).astype(BF16), d_query) for (own, _), arrived in zip(far, far_arrived)
    ]
    chip_arrived = [places.send(part, "chips", -(k + 1)) for k, part in enumerate(far_sums)]
    outgoing = behind.finish((d_query, far_sums, sum_out))
    out_mate = places.send(tied(out_mate, d_query), "core", 1)
    sum_out = members_sum(tied(sum_out, behind.sent))[0]
    outgoing = tied(outgoing, sum_out)
    d_normed_part = pl.pallas_call(
        dots_back_kernel,
        grid=(seqs,),
        in_specs=[rows_of(length), rows_of(length), whole((2, D, D))],
        out_specs=rows_of(length),
        out_shape=wide,
        compiler_params=params(),
        cost_estimate=cost(4 * count * D * D, 10 * count * D),
        name="normed_back",
    )(*tied((d_query, d_gate), behind.sent), full_qg)
    outgoing = tied(outgoing, d_normed_part)

    d_kv, mix_grads = pl.pallas_call(
        lambda *refs: state_back_kernel(seqs, *refs),
        grid=(tiles,),
        in_specs=[cols(count)] * 5
        + [tile_state, cols(length), whole((count, D)), pl.BlockSpec(memory_space=pl.ANY)],
        out_specs=[pl.BlockSpec((2, count, TILE), lambda i: (0, 0, i)), pair_cols],
        out_shape=[jax.ShapeDtypeStruct((2, count, D), BF16), four_grads],
        input_output_aliases={8: 1},
        compiler_params=params(),
        cost_estimate=cost(5 * count * D * D, 18 * count * D),
        name="state_back",
    )(keys, values, pre_k, d_key_part, d_value_part, outgoing, trail, normed, mix_grads)
    wide_total = summed(near, *near_arrived, *chip_arrived).astype(BF16)
    sum_out = padded(sum_out, w_down.shape[0] // places.members)
    wide_blocks = jnp.stack([wide_total[2], wide_total[0], wide_total[1], sum_out])
    wide_parts = places.scattered(wide_blocks, "quads")
    mix_sums = scattered(tied(mix_grads, chip_arrived))
    activations = (tied(sums[0], wide_blocks) + out_mate.astype(F32)).astype(BF16)
    d_kv = tied(d_kv, wide_blocks)

    input_grad = pl.pallas_call(
        input_back_kernel,
        grid=(seqs,),
        in_specs=[
            pl.BlockSpec((2, length, D), lambda i: (0, i, 0)),
            whole((2, D, D)),
            rows_of(length),
            rows_of(length),
            rows_of(length),
        ],
        out_specs=rows_of(length),
        out_shape=narrow,
        compiler_params=params(),
        cost_estimate=cost(4 * count * D * D, 16 * count * D),
        name="input_back",
    )(d_kv, full_kv, d_normed_part, x, d_middle).reshape(tokens.shape)

    wide_mom = ((m_down[None], 0), (m_in, 0), (m_in, 1), (m_out[None], 0))
    mix_mom = [(m_mix, i) for i in range(4)]

    def momentum_rows(sources, grad, after):
        arrays = tied([array for array, _ in sources], after)
        own = own_rows(places, [(array, at) for array, (_, at) in zip(arrays, sources)], grad.shape[0])
        return (MOMENTUM * own + grad.astype(F32)).astype(BF16)

    def to_members(part):
        return [places.send(part, "members", j) for j in range(1, places.members)]

    mix_split = tied(mix_sums, (input_grad, wide_parts)).reshape(4, places.members, -1, D)
    mix_offers = [
        lax.dynamic_index_in_dim(mix_split, (places.member + j) % places.members, 1, False)
        for j in range(places.members)
    ]
    mix_arrived = [places.send(part, "members", j) for j, part in enumerate(mix_offers[1:], 1)]
    wide_grad = summed(*tied(wide_parts, (activations, mix_offers))).astype(BF16)

    wide_low = momentum_rows(wide_mom, wide_grad, wide_blocks)
    wide_known = [wide_low] + to_members(wide_low)
    wide_far = [places.send(wide_low, "chips", k) for k in range(1, places.chips)]
    wide_first = places.send(tied(wide_grad, wide_low), "quads", 1)
    mix_sums = summed(*tied([mix_offers[0]] + mix_arrived, wide_low)).astype(BF16)
    mix_blocks = tied(jnp.stack([mix_sums[i] for i in (2, 0, 1, 3)]), wide_far)
    mix_parts = places.scattered(mix_blocks, "quads")
    mix_grad = summed(*mix_parts).astype(BF16)
    wide_last = [other for part in wide_far for other in to_members(part)]
    wide_known, wide_far = tied((wide_known, wide_far), (mix_parts, wide_last))
    wide_core = jnp.concatenate(wide_known + wide_far, axis=0)
    wide_every = [wide_core, places.send(wide_core, "core", 1)] + wide_last
    wide_every += [places.send(part, "core", 1) for part in wide_last]

    mix_low = momentum_rows(mix_mom, mix_grad, wide_blocks)
    rows, own = wide_grad.shape[0], mix_grad.shape[0]
    mix_others = to_members(jnp.concatenate([mix_low, mix_grad], axis=0))
    mix_known = jnp.concatenate([mix_low] + [part[:own] for part in mix_others], axis=0)
    mix_every = lax.all_gather(mix_known, "batch", axis=0, tiled=True)

    wide_all, mix_all = Blocks(places, rows), Blocks(places, own)
    wide_all.add(wide_grad, (0, 0, 0))
    wide_all.add(wide_first, (0, 1, 0))
    mix_all.add(mix_grad, (0, 0, 0))
    for j, part in enumerate(mix_others, 1):
        mix_all.add(part, (own, 0, j))
    both = jnp.concatenate([wide_grad, mix_grad], axis=0)
    mix_first = places.send(tied(mix_grad, mix_low), "quads", 1)
    second = places.send(tied(both, (mix_low, mix_first)), "quads", 2)
    early = jnp.concatenate(tied([wide_grad, wide_first], mix_known), axis=0)
    early_arrived = to_members(early)
    for j, part in enumerate(early_arrived, 1):
        wide_all.add(part, (0, 0, j), (rows, 1, j))

    wide_rows, wide_rest = newton_rows(tied(wide_every, (early, mix_known)), wide_core[: rows * places.members], rows)
    wide_x, mix_x = Blocks(places, rows), Blocks(places, own)
    wide_x.add(wide_rows, (0, 0, 0))
    wide_x.add(wide_rest, *[((j - 1) * rows, 0, j) for j in range(1, places.members)])
    second, mix_first = tied((second, mix_first), wide_rows)
    nearer = jnp.concatenate([second, mix_first], axis=0)
    nearer_arrived = to_members(nearer)
    wide_all.add(second, (0, 2, 0))
    mix_all.add(second, (rows, 2, 0))
    mix_all.add(mix_first, (0, 1, 0))
    for j, part in enumerate(nearer_arrived, 1):
        wide_all.add(part, (0, 2, j))
        mix_all.add(part, (rows, 2, j), (rows + own, 1, j))
    x_sent = tied(wide_rows, mix_every)
    x_parts = [places.send(x_sent, "quads", k) for k in (1, 2)]
    mix_rows, mix_rest = newton_rows([tied(mix_every, (wide_rows, early_arrived, nearer))], mix_known, own)
    x_pair = jnp.concatenate(tied(x_parts, (mix_rows, nearer_arrived)), axis=0)
    third = places.send(tied(both, x_pair), "quads", 3)
    x_parts.append(places.send(tied(x_sent, x_pair), "quads", 3))
    for k, part in enumerate(x_parts, 1):
        wide_x.add(part, (0, k, 0))
    x_arrived = to_members(x_pair)
    for j, part in enumerate(x_arrived, 1):
        wide_x.add(part, (0, 1, j), (rows, 2, j))
    wide_all.add(third, (0, 3, 0))
    mix_all.add(third, (rows, 3, 0))
    for j, part in enumerate(to_members(third), 1):
        wide_all.add(part, (0, 3, j))
        mix_all.add(part, (rows, 3, j))
    mix_x.add(mix_rows, (0, 0, 0))
    mix_x.add(mix_rest, *[((j - 1) * own, 0, j) for j in range(1, places.members)])
    mix_sent = tied(mix_rows, x_arrived)
    mix_parts = [places.send(mix_sent, "quads", k) for k in (1, 2, 3)]
    x_last = to_members(tied(x_parts[2], third))
    for j, part in enumerate(x_last, 1):
        wide_x.add(part, (0, 3, j))
    for k, part in enumerate(mix_parts, 1):
        mix_x.add(part, (0, k, 0))
    for j, part in enumerate(to_members(jnp.concatenate(tied(mix_parts, x_last), axis=0)), 1):
        mix_x.add(part, *[((k - 1) * own, k, j) for k in (1, 2, 3)])

    hidden_rows, width_rows = w_down.shape[0] // places.members, w_out.shape[0] // places.members
    wide_groups = [(0, None, hidden_rows), (1, 0, hidden_rows), (1, 1, hidden_rows), (2, None, width_rows)]
    mix_groups = [(0, i, width_rows) for i in range(4)]
    ones = [1.0] * 4
    factor = math.sqrt(FF / D)
    steps = [-STEP_RATE, -STEP_RATE * factor, -STEP_RATE * factor, -STEP_RATE]
    new_down, new_in, new_out, copy_down, copy_in, copy_out = wide_x.finished(
        (w_down, w_in, w_out), wide_groups, (1.0, steps), True
    )
    mom_down, mom_in, mom_out = wide_all.finished(
        (m_down, m_in, m_out), wide_groups, (MOMENTUM, ones), late=new_in
    )
    (mom_mix,) = mix_all.finished((m_mix,), mix_groups, (MOMENTUM, ones), late=mom_in)
    new_mix, copy_mix = mix_x.finished((w_mix,), mix_groups, (1.0, [-STEP_RATE] * 4), True, late=mom_mix)
    return (
        activations.reshape(tokens.shape),
        input_grad,
        mom_mix,
        mom_out,
        mom_in,
        mom_down,
        new_mix,
        new_out,
        new_in,
        new_down,
        copy_mix,
        copy_out,
        copy_in,
        copy_down,
    )


def solution(mesh):
    batch_rows = P(None, "batch", None)
    flat_rows = P("batch", None)
    block = P("batch", "seq", None)
    four = (batch_rows, flat_rows, batch_rows, flat_rows)
    in_specs = (block, block, P(None, "seq")) + four + four
    out_specs = (block, block) + four + four + four
    return jax.shard_map(shards, mesh=mesh, in_specs=in_specs, out_specs=out_specs, check_vma=False)
```

```python
import math

import jax
import jax.numpy as jnp
from jax import lax
from jax.experimental import pallas as pl
from jax.experimental.pallas import tpu as pltpu
from jax.sharding import PartitionSpec as P

D = 1024
HEAD_COUNT = 16
HEAD_DIM = 64
FF = 2816
ITERS = 5
PAIRS = HEAD_COUNT // 2
LANES = 2 * HEAD_DIM
TILE = 256
HEADS_PER_TILE = TILE // HEAD_DIM
PAIRS_PER_TILE = TILE // LANES
QUADS = 4

EPSILON = 1e-06
NORM_FLOOR = 1e-07
COEFF_A = 3.4445
COEFF_B = -4.775
COEFF_C = 2.0315
MOMENTUM = 0.5
STEP_RATE = 0.8

F32 = jnp.float32
BF16 = jnp.bfloat16
MIB = 1024 * 1024


def dot_nn(left, right):
    return lax.dot_general(left, right, (((1,), (0,)), ((), ())), preferred_element_type=F32)


def dot_nt(left, right):
    return lax.dot_general(left, right, (((1,), (1,)), ((), ())), preferred_element_type=F32)


def dot_tn(left, right):
    return lax.dot_general(left, right, (((0,), (0,)), ((), ())), preferred_element_type=F32)


def silu_grad(inputs):
    sigma = jax.nn.sigmoid(inputs)
    return sigma * (1.0 + inputs * (1.0 - sigma))


def inverse_rms(inputs):
    return lax.rsqrt(jnp.mean(inputs * inputs, axis=-1, keepdims=True) + EPSILON)


def normalize_back(inputs, grad):
    factor = inverse_rms(inputs)
    normed = inputs * factor
    return factor * (grad - normed * jnp.mean(grad * normed, axis=-1, keepdims=True))


def first_half(shape):
    return lax.broadcasted_iota(jnp.int32, shape, len(shape) - 1) < HEAD_DIM


def head_parts(pair):
    low = first_half(pair.shape)
    zero = jnp.zeros_like(pair)
    return (jnp.where(low, pair, zero), jnp.where(low, zero, pair))


def compact(full):
    return jnp.where(first_half((HEAD_DIM, LANES)), full[:HEAD_DIM], full[HEAD_DIM:])


def expand(state):
    return jnp.concatenate(head_parts(state), axis=0)


def params(limit=56):
    return pltpu.CompilerParams(vmem_limit_bytes=limit * MIB)


def cost(flops, nbytes, share=0.1):
    return pl.CostEstimate(flops=int(flops / share), bytes_accessed=int(nbytes / share), transcendentals=0)


def whole(shape):
    return pl.BlockSpec(shape, lambda i: (0,) * len(shape))


def cols(rows, width=TILE):
    return pl.BlockSpec((rows, width), lambda i: (0, i))


def rows_of(rows, width=D):
    return pl.BlockSpec((rows, width), lambda i: (i, 0))


def exact(left, right, dims):
    return lax.dot_general(
        left, right, (dims, ((), ())), preferred_element_type=F32, precision=lax.Precision.HIGHEST
    )


def decay_kernel(log_ref, last_ref, cum_ref, lead_ref, trail_ref, mask_ref, mask_t_ref):
    logs = log_ref[...]
    length = logs.shape[1]
    row = lax.broadcasted_iota(jnp.int32, (length, length), 0)
    col = lax.broadcasted_iota(jnp.int32, (length, length), 1)
    cum = exact(logs, (row <= col).astype(F32), ((1,), (0,)))
    cum_ref[...] = cum
    last = cum[:, length - 1 :]
    last_ref[...] = last
    lane = lax.broadcasted_iota(jnp.int32, (HEAD_COUNT, D), 1) // HEAD_DIM
    spread = (lane == lax.broadcasted_iota(jnp.int32, (HEAD_COUNT, D), 0)).astype(F32)
    lead_ref[...] = jnp.exp(exact(cum, spread, ((0,), (0,))))
    trail_ref[...] = jnp.exp(exact(last - cum, spread, ((0,), (0,))))
    upright = cum.T
    for h in range(HEAD_COUNT):
        span = upright[:, h : h + 1] - cum[h : h + 1, :]
        mask_ref[h] = jnp.where(row >= col, jnp.exp(jnp.minimum(span, 0.0)), 0.0)
        mask_t_ref[h] = jnp.where(col >= row, jnp.exp(jnp.minimum(-span, 0.0)), 0.0)


def factor_kernel(members, place_ref, logs_ref, out_ref):
    logs = logs_ref[...]
    count = logs.shape[0]
    quad, member = place_ref[0], place_ref[1]
    here = quad * members + member
    start, end = quad * members, quad * members + members - 1
    row = lax.broadcasted_iota(jnp.int32, (count, count), 0)
    col = lax.broadcasted_iota(jnp.int32, (count, count), 1)
    before = exact((col < row).astype(F32), logs, ((1,), (0,)))
    through = before + logs
    at_row = lax.broadcasted_iota(jnp.int32, (count, HEAD_COUNT), 0)

    def at(sums, i):
        return jnp.sum(jnp.where(at_row == i, sums, 0.0), axis=0, keepdims=True)

    def factor(log, valid=True):
        return jnp.where(valid, jnp.exp(jnp.minimum(log, 0.0)), 0.0)

    rows = []
    for backward in (False, True):
        for k in range(1, QUADS):
            if backward:
                rows.append(factor(at(before, here + k * members) - at(through, end), quad + k < QUADS))
            else:
                rows.append(factor(at(before, start) - at(through, here - k * members), quad - k >= 0))
        spots = [lax.rem(member + k, members) for k in range(members)]
        for spot in spots:
            there = start + spot
            rows.append(factor(at(through, end) - at(through, there) if backward else at(before, there) - at(before, start)))
        for spot in spots:
            there = start + spot
            if backward:
                rows.append(factor(at(before, here) - at(through, there), spot < member))
            else:
                rows.append(factor(at(before, there) - at(through, here), spot > member))
    lane = lax.broadcasted_iota(jnp.int32, (HEAD_COUNT, D), 1) // HEAD_DIM
    spread = (lane == lax.broadcasted_iota(jnp.int32, (HEAD_COUNT, D), 0)).astype(F32)
    out_ref[...] = exact(jnp.concatenate(rows, axis=0), spread, ((1,), (0,)))


def kv_kernel(seqs, x_ref, w_ref, trail_ref, normed_ref, pk_ref, k_ref, v_ref, state_ref):
    @pl.when(pl.program_id(0) == 0)
    def _():
        inputs = x_ref[...].astype(F32)
        normed_ref[...] = (inputs * inverse_rms(inputs)).astype(BF16)

    normed = normed_ref[...]
    pre_k = dot_nn(normed, w_ref[0])
    keys = pre_k * jax.nn.sigmoid(pre_k)
    values = dot_nn(normed, w_ref[1]).astype(BF16)
    pk_ref[...] = pre_k.astype(BF16)
    k_ref[...] = keys.astype(BF16)
    v_ref[...] = values
    trail = trail_ref[...]
    length = trail.shape[0]
    for b in range(seqs):
        at = slice(b * length, (b + 1) * length)
        scaled = (keys[at] * trail).astype(BF16)
        for p in range(PAIRS_PER_TILE):
            lanes = slice(p * LANES, (p + 1) * LANES)
            state_ref[b, p] = compact(dot_tn(scaled[:, lanes], values[at, lanes])).astype(BF16)


def q_kernel(seqs, normed_ref, w_ref, k_ref, v_ref, mask_ref, pq_ref, q_ref, pg_ref, o_ref):
    normed = normed_ref[...]
    pre_q = dot_nn(normed, w_ref[0])
    pq_ref[...] = pre_q.astype(BF16)
    q_ref[...] = (pre_q * jax.nn.sigmoid(pre_q)).astype(BF16)
    pg_ref[...] = dot_nn(normed, w_ref[1]).astype(BF16)
    length = mask_ref.shape[1]
    for b in range(seqs):
        at = slice(b * length, (b + 1) * length)
        for p in range(PAIRS_PER_TILE):
            lanes = slice(p * LANES, (p + 1) * LANES)
            q_parts = head_parts(q_ref[at, lanes])
            v_parts = head_parts(v_ref[at, lanes])
            keys = k_ref[at, lanes]
            total = jnp.zeros((length, LANES), F32)
            for h in range(2):
                scores = dot_nt(q_parts[h], keys) * mask_ref[2 * p + h]
                total = total + dot_nn(scores.astype(BF16), v_parts[h])
            o_ref[at, lanes] = total


def mid_kernel(o_ref, q_ref, state_ref, lead_ref, pg_ref, x_ref, wo_ref, att_ref, hid_ref, mid_ref, nf_ref):
    scaled = (q_ref[...].astype(F32) * lead_ref[...]).astype(BF16)
    for p in range(PAIRS):
        lanes = slice(p * LANES, (p + 1) * LANES)
        att_ref[:, lanes] = o_ref[:, lanes] + dot_nn(scaled[:, lanes], expand(state_ref[0, p]))
    attended = att_ref[...]
    gate_in = pg_ref[...].astype(F32)
    hidden = (attended * inverse_rms(attended) * gate_in * jax.nn.sigmoid(gate_in)).astype(BF16)
    hid_ref[...] = hidden
    middle = x_ref[...].astype(F32) + dot_nn(hidden, wo_ref[...])
    mid_ref[...] = middle
    nf_ref[...] = (middle * inverse_rms(middle)).astype(BF16)


def ffn_kernel(carry, last, more, cut, place_ref, x_refs, out_refs, buffers, sems):
    nf_buf, cot_buf, w_in_buf, w_down_buf, out_buf, dn_buf, prod_buf, first_buf, second_buf, grad_buf = buffers[:10]
    rows = grad_buf.shape[1]
    if place_ref is None:
        targets = [nf_buf, w_in_buf, cot_buf, w_down_buf]
    else:
        half = rows // 2
        here = pl.ds(pl.multiple_of(place_ref[0] * half, half), half)
        there = pl.ds(pl.multiple_of((1 - place_ref[0]) * half, half), half)
        targets = [nf_buf, w_in_buf.at[:, here], w_in_buf.at[:, there], cot_buf, w_down_buf.at[here], w_down_buf.at[there]]
    needed = len(targets)
    targets = targets + [out_buf, dn_buf][:carry] + ([grad_buf] if more else [])
    loads = [
        pltpu.make_async_copy(source, target, sems.at[i]) for i, (source, target) in enumerate(zip(x_refs, targets))
    ]
    for load in loads:
        load.start()
    sum_bufs = buffers[10:] if last else (out_buf, dn_buf)
    out_copies = [pltpu.make_async_copy(buf, ref, sems.at[9 + i]) for i, (buf, ref) in enumerate(zip(sum_bufs, out_refs))]
    pieces = [pl.ds(0, cut), pl.ds(cut, rows - cut)] if cut else [pl.ds(0, rows)]
    grad_copies = [
        [
            pltpu.make_async_copy(grad_buf.at[i, piece], out_refs[2 + j].at[i], sems.at[11 + 2 * i + j])
            for j, piece in enumerate(pieces)
        ]
        for i in range(3)
    ]
    count = nf_buf.shape[0]
    first_half = 2 if place_ref is None else 3
    step = min(TILE, count)
    for at in [slice(t, t + step) for t in range(0, count, step)]:
        if at.start == 0:
            for load in loads[:first_half]:
                load.wait()
        normed = nf_buf[at, :]
        first = dot_nt(w_in_buf[0], normed)
        second = dot_nt(w_in_buf[1], normed)
        if at.start == 0:
            for load in loads[first_half:needed]:
                load.wait()
        cot = cot_buf[at, :]
        d_product = dot_nt(w_down_buf[...], cot)
        product = (first * second).astype(BF16)
        d_first = (d_product * second).astype(BF16)
        d_second = (d_product * first).astype(BF16)
        prod_buf[:, at] = product
        first_buf[:, at] = d_first
        second_buf[:, at] = d_second
        out = dot_tn(product, w_down_buf[...])
        d_normed = dot_tn(d_first, w_in_buf[0]) + dot_tn(d_second, w_in_buf[1])
        if at.start == 0:
            for load in loads[needed:]:
                load.wait()
        if carry > 0:
            out = out_buf[at, :] + out
        if carry > 1:
            d_normed = dn_buf[at, :] + d_normed
        sum_bufs[0][at, :] = out.astype(sum_bufs[0].dtype)
        sum_bufs[1][at, :] = d_normed.astype(sum_bufs[1].dtype)
    for copy in out_copies:
        copy.start()
    for i, (left, right) in enumerate(((first_buf, nf_buf), (second_buf, nf_buf), (prod_buf, cot_buf))):
        for at in [slice(c, c + TILE) for c in range(0, D, TILE)]:
            grad = dot_nn(left[...], right[:, at])
            if more:
                grad = grad + grad_buf[i, :, at].astype(F32)
            grad_buf[i, :, at] = grad.astype(BF16)
        for copy in grad_copies[i]:
            copy.start()
    for copy in out_copies + [copy for copies in grad_copies for copy in copies]:
        copy.wait()


def ffn(normed, cot, weights, sums=(), last=False, grads=None, cut=0, place=None):
    w_in, w_down = ((w,) if place is None else w for w in weights)
    count, rows = normed.shape[0], sum(part.shape[0] for part in w_down)
    away = pl.BlockSpec(memory_space=pl.ANY)
    kind = BF16 if last else F32
    ins = (normed, *w_in, cot, *w_down, *sums) + (() if grads is None else (grads,))
    places = () if place is None else (place,)
    n_in = len(ins)
    parts = [cut, rows - cut] if cut else [rows]
    n_out = 2 + len(parts)
    has_grads = grads is not None

    def body(*refs):
        place_ref = refs[0] if places else None
        refs = refs[len(places) :]
        outs, buffers = refs[n_in : n_in + n_out], refs[n_in + n_out : -1]
        ffn_kernel(len(sums), last, has_grads, cut, place_ref, refs[:n_in], outs, buffers, refs[-1])

    tokens_by = pltpu.VMEM((count, D), BF16)
    units_by = pltpu.VMEM((rows, count), BF16)
    out, d_normed, *grads = pl.pallas_call(
        body,
        in_specs=[pl.BlockSpec(memory_space=pltpu.SMEM)] * len(places) + [away] * n_in,
        out_specs=[away] * n_out,
        out_shape=[jax.ShapeDtypeStruct((count, D), kind)] * 2
        + [jax.ShapeDtypeStruct((3, part, D), BF16) for part in parts],
        scratch_shapes=[tokens_by, tokens_by, pltpu.VMEM((2, rows, D), BF16), pltpu.VMEM((rows, D), BF16)]
        + [pltpu.VMEM((count, D), F32)] * 2
        + [units_by] * 3
        + [pltpu.VMEM((3, rows, D), BF16)]
        + ([tokens_by] * 2 if last else [])
        + [pltpu.SemaphoreType.DMA((17,))],
        compiler_params=params(60),
        cost_estimate=cost(16 * count * D * rows, 12 * rows * D + 12 * count * D),
        name="ffn",
    )(*places, *ins)
    return (out, d_normed), grads


def gate_back_kernel(
    dn_ref, dn_mate_ref, mid_ref, cot_ref, wo_ref, att_ref, pg_ref, q_ref, lead_ref, *out_refs
):
    dmid_ref, datt_ref, dgate_ref, state_ref = out_refs
    d_normed_ffn = dn_ref[...] + dn_mate_ref[...].astype(F32)
    d_middle = cot_ref[...].astype(F32) + normalize_back(mid_ref[...], d_normed_ffn)
    d_middle = d_middle.astype(BF16)
    dmid_ref[...] = d_middle
    d_hidden = dot_nt(d_middle, wo_ref[...])
    attended = att_ref[...]
    factor = inverse_rms(attended)
    out_norm = attended * factor
    gate_in = pg_ref[...].astype(F32)
    sigma = jax.nn.sigmoid(gate_in)
    dgate_ref[...] = (d_hidden * out_norm * sigma * (1.0 + gate_in * (1.0 - sigma))).astype(BF16)
    grad = d_hidden * gate_in * sigma
    d_att = factor * (grad - out_norm * jnp.mean(grad * out_norm, axis=-1, keepdims=True))
    d_att = d_att.astype(BF16)
    datt_ref[...] = d_att
    scaled = (q_ref[...].astype(F32) * lead_ref[...]).astype(BF16)
    for p in range(PAIRS):
        lanes = slice(p * LANES, (p + 1) * LANES)
        state_ref[0, p] = compact(dot_tn(scaled[:, lanes], d_att[:, lanes])).astype(BF16)


def early_grads_kernel(hid_ref, nf_ref, dmid_ref, dgate_ref, out_grad_ref, gate_grad_ref):
    out_grad_ref[0] = dot_tn(hid_ref[...], dmid_ref[...]).astype(BF16)
    gate_grad_ref[0] = dot_tn(nf_ref[...], dgate_ref[...]).astype(BF16)


def att_back_kernel(
    seqs, q_ref, k_ref, v_ref, da_ref, pq_ref, mask_ref, mask_t_ref, state_ref, lead_ref, nf_ref, *out_refs
):
    dq_ref, dk_ref, dv_ref, grad_ref = out_refs[1:]
    lead = lead_ref[...]
    length = lead.shape[0]
    for b in range(seqs):
        at = slice(b * length, (b + 1) * length)
        for p in range(PAIRS_PER_TILE):
            lanes = slice(p * LANES, (p + 1) * LANES)
            queries, keys, values, d_att = (r[at, lanes] for r in (q_ref, k_ref, v_ref, da_ref))
            q_parts, k_parts, v_parts, d_parts = (head_parts(a) for a in (queries, keys, values, d_att))
            d_q = dot_nt((d_att.astype(F32) * lead[:, lanes]).astype(BF16), expand(state_ref[b, p]))
            d_k = jnp.zeros((length, LANES), F32)
            d_v = jnp.zeros((length, LANES), F32)
            for h in range(2):
                mask, mask_t = mask_ref[2 * p + h], mask_t_ref[2 * p + h]
                d_scores = (dot_nt(d_parts[h], values) * mask).astype(BF16)
                d_scores_t = (dot_nt(v_parts[h], d_att) * mask_t).astype(BF16)
                scores_t = (dot_nt(k_parts[h], queries) * mask_t).astype(BF16)
                d_q = d_q + dot_nn(d_scores, k_parts[h])
                d_k = d_k + dot_nn(d_scores_t, q_parts[h])
                d_v = d_v + dot_nn(scores_t, d_parts[h])
            dq_ref[at, lanes] = (d_q * silu_grad(pq_ref[at, lanes].astype(F32))).astype(BF16)
            dk_ref[at, lanes] = d_k
            dv_ref[at, lanes] = d_v
    grad_ref[0] = dot_tn(nf_ref[...], dq_ref[...]).astype(BF16)


def state_back_kernel(
    seqs, k_ref, v_ref, pk_ref, dk_in_ref, dv_in_ref, state_ref, trail_ref, nf_ref, _, dkv_ref, grad_ref
):
    trail = trail_ref[...]
    length = trail.shape[0]
    for b in range(seqs):
        at = slice(b * length, (b + 1) * length)
        k_scaled = (k_ref[at, :].astype(F32) * trail).astype(BF16)
        v_scaled = (v_ref[at, :].astype(F32) * trail).astype(BF16)
        for p in range(PAIRS_PER_TILE):
            lanes = slice(p * LANES, (p + 1) * LANES)
            state = expand(state_ref[b, p])
            d_k = dk_in_ref[at, lanes] + dot_nt(v_scaled[:, lanes], state)
            d_v = dv_in_ref[at, lanes] + dot_nn(k_scaled[:, lanes], state)
            dkv_ref[0, at, lanes] = (d_k * silu_grad(pk_ref[at, lanes].astype(F32))).astype(BF16)
            dkv_ref[1, at, lanes] = d_v.astype(BF16)
    for i in range(2):
        grad_ref[i] = dot_tn(nf_ref[...], dkv_ref[i]).astype(BF16)


def dots_back_kernel(dq_ref, dg_ref, w_ref, out_ref):
    out_ref[...] = dot_nt(dq_ref[...], w_ref[0]) + dot_nt(dg_ref[...], w_ref[1])


def input_back_kernel(dkv_ref, w_ref, part_ref, x_ref, dmid_ref, out_ref):
    d_normed = part_ref[...] + dot_nt(dkv_ref[0], w_ref[0]) + dot_nt(dkv_ref[1], w_ref[1])
    d_tokens = dmid_ref[...].astype(F32) + normalize_back(x_ref[...].astype(F32), d_normed)
    out_ref[...] = d_tokens.astype(BF16)


def newton_kernel(parts, *refs):
    b_refs, (row_ref, out_ref, rest_ref, g_ref, gb_ref, nb_ref, h_ref, hb_ref, x_ref) = refs[:parts], refs[parts:]
    tiles = [slice(i * TILE, (i + 1) * TILE) for i in range(D // TILE)]

    def right_of(at):
        return slice(at.start, D)

    def mirrored(target, at, part):
        low = part.astype(BF16)
        target[at, right_of(at)] = low
        for other in tiles:
            if other.start > at.start:
                target[other, at] = low[:, other.start - at.start : other.stop - at.start].T

    trace = jnp.zeros((1, 1), F32)
    for at in tiles:
        part = sum(dot_tn(b_ref[:, at], b_ref[:, right_of(at)]) for b_ref in b_refs)
        g_ref[at, right_of(at)] = part
        on_row = lax.broadcasted_iota(jnp.int32, (TILE, TILE), 0)
        on_col = lax.broadcasted_iota(jnp.int32, (TILE, TILE), 1)
        trace = trace + jnp.sum(jnp.where(on_row == on_col, part[:, :TILE], 0.0), keepdims=True)
    inverse = 1.0 / (jnp.sqrt(trace) + NORM_FLOOR)
    x_ref[...] = row_ref[...].astype(F32) * inverse
    scale = inverse * inverse
    for at in tiles:
        gram = g_ref[at, right_of(at)] * scale
        g_ref[at, right_of(at)] = gram
        mirrored(gb_ref, at, gram)

    def polynomial():
        for at in tiles:
            square = dot_nn(gb_ref[at, :], gb_ref[:, right_of(at)])
            mirrored(nb_ref, at, COEFF_B * g_ref[at, right_of(at)] + COEFF_C * square)
        state = x_ref[...]
        x_ref[...] = COEFF_A * state + dot_nn(state.astype(BF16), nb_ref[...])

    @pl.loop(0, ITERS - 1)
    def _(turn):
        polynomial()
        for at in tiles:
            half = COEFF_A * g_ref[at, right_of(at)] + dot_nn(gb_ref[at, :], nb_ref[:, right_of(at)])
            h_ref[at, right_of(at)] = half
            mirrored(hb_ref, at, half)
        for at in tiles:
            gram = COEFF_A * h_ref[at, right_of(at)] + dot_nn(nb_ref[at, :], hb_ref[:, right_of(at)])
            g_ref[at, right_of(at)] = gram
            mirrored(gb_ref, at, gram)

    polynomial()
    own = out_ref.shape[0]
    out_ref[...] = x_ref[:own, :].astype(BF16)
    rest_ref[...] = x_ref[own:, :].astype(BF16)


def newton_rows(every, mine, first):
    rows, own = sum(part.shape[0] for part in every), mine.shape[0]
    return pl.pallas_call(
        lambda *refs: newton_kernel(len(every), *refs),
        out_shape=[jax.ShapeDtypeStruct((first, D), BF16), jax.ShapeDtypeStruct((own - first, D), BF16)],
        grid=(1,),
        in_specs=[whole(part.shape) for part in every] + [whole((own, D))],
        out_specs=[whole((first, D)), whole((own - first, D))],
        scratch_shapes=[
            pltpu.VMEM((D, D), F32),
            pltpu.VMEM((D, D), BF16),
            pltpu.VMEM((D, D), BF16),
            pltpu.VMEM((D, D), F32),
            pltpu.VMEM((D, D), BF16),
            pltpu.VMEM((own, D), F32),
        ],
        compiler_params=params(),
        cost_estimate=cost(2 * D * D * (13 * D + rows + 5 * own), 2 * D * (rows + 2 * own)),
        name="newton",
    )(*every, mine)


class Places:
    def __init__(self):
        self.members = lax.axis_size("seq") // QUADS
        self.chips = lax.axis_size("batch") // 2
        at = lax.axis_index("seq").astype(jnp.uint32)
        self.quad, self.member = at // self.members, at % self.members
        at = lax.axis_index("batch").astype(jnp.uint32)
        self.chip, self.core = at // 2, at % 2

    def level(self, name):
        return {
            "quads": (QUADS, self.quad),
            "members": (self.members, self.member),
            "chips": (self.chips, self.chip),
            "core": (2, self.core),
        }[name]

    def send(self, value, name, k, wrap=True):
        pairs = []
        if name in ("quads", "members"):
            for q in range(QUADS):
                for m in range(self.members):
                    if name == "members":
                        pairs.append((q * self.members + m, q * self.members + (m + k) % self.members))
                    elif wrap or 0 <= q + k < QUADS:
                        pairs.append((q * self.members + m, (q + k) % QUADS * self.members + m))
            return lax.ppermute(value, "seq", pairs)
        for x in range(self.chips):
            for c in range(2):
                to = 2 * x + (c + k) % 2 if name == "core" else (x + k) % self.chips * 2 + c
                pairs.append((2 * x + c, to))
        return lax.ppermute(value, "batch", pairs)

    def pair(self, value):
        pairs = []
        for q in range(QUADS):
            for m in range(self.members):
                pairs.append((q * self.members + m, (q ^ 1) * self.members + m))
        return lax.ppermute(value, "seq", pairs)

    def scattered(self, blocks, name, axis=0):
        count, mine = self.level(name)

        def block(j):
            return lax.dynamic_index_in_dim(blocks, j, axis, False)

        return [block(mine)] + [self.send(block((mine + k) % count), name, k) for k in range(1, count)]

    def scatter(self, blocks, name, axis=0):
        return summed(*self.scattered(blocks, name, axis)).astype(BF16)

    def gather(self, block, name, axis=0):
        count, mine = self.level(name)
        shape = block.shape[:axis] + (count,) + block.shape[axis:]
        result = jnp.zeros(shape, block.dtype)
        result = lax.dynamic_update_index_in_dim(result, block, mine, axis)
        for k in range(1, count):
            part = self.send(block, name, k)
            result = lax.dynamic_update_index_in_dim(result, part, (mine + (count - k)) % count, axis)
        return result

    def far_rows(self, own, after, pair_after, use_after):
        n, rows, _ = own.shape
        split = own.reshape(n, 2, rows // 2, D)
        mine = tied(lax.dynamic_index_in_dim(split, self.quad % 2, 1, False), after)
        far = []
        for k in range(1, self.chips):
            part = tied(self.send(mine, "chips", k), pair_after)
            far.append(tied((part, self.pair(part)), use_after))
        return far


def tied(value, *others):
    return lax.optimization_barrier((value, others))[0]


class Carried:
    def __init__(self, places, local, factors, backward):
        self.places = places
        factors = factors.reshape(-1, PAIRS, 1, LANES)
        self.quad_factors = factors[: QUADS - 1]
        self.spot_factors = factors[QUADS - 1 : QUADS - 1 + places.members]
        self.local_factors = factors[QUADS - 1 + places.members :]
        self.local = local
        sign = -1 if backward else 1
        self.arrived = [places.send(self.local, "quads", sign * k, wrap=False) for k in range(1, QUADS)]

    def finish(self, after=()):
        outer = sum(part.astype(F32) * self.quad_factors[k] for k, part in enumerate(self.arrived))
        local = self.local.astype(F32)
        own = self.spot_factors[0] * outer
        self.sent = [
            tied((self.spot_factors[k] * outer + self.local_factors[k] * local).astype(BF16), after)
            for k in range(1, self.places.members)
        ]
        parts = [self.places.send(part, "members", k) for k, part in enumerate(self.sent, 1)]
        return summed(own, *parts).astype(BF16)


def padded(block, rows):
    return jnp.pad(block, ((0, rows - block.shape[0]), (0, 0)))


def summed(*parts):
    total = parts[0].astype(F32)
    for part in parts[1:]:
        total = total + part.astype(F32)
    return total


class WideSum:
    def __init__(self, places, rows):
        self.places = places
        self.shape = (3, places.members, rows // places.members, D)

    def ordered(self, weights):
        places = self.places
        split = weights.reshape(weights.shape[0], places.members, -1, D)
        parts = [
            lax.dynamic_index_in_dim(split, (places.member + k) % places.members, 1, False)
            for k in range(places.members)
        ]
        return jnp.concatenate(parts, axis=1).astype(BF16)

    def cut(self):
        own = self.shape[2]
        return own if own % 16 == 0 else 0

    def parts(self, grads):
        if len(grads) == 1:
            split = grads[0].reshape(self.shape)
            return split[:, 0], [split[:, k] for k in range(1, self.places.members)]
        split = grads[1].reshape((3, -1) + self.shape[2:])
        if self.places.members == 2:
            return grads[0], [grads[1]]
        return grads[0], [split[:, k] for k in range(self.places.members - 1)]

    def exchange(self, offers):
        return [self.places.send(offer, "members", k + 1) for k, offer in enumerate(offers)]


def place_kernel(members, rows, sources, place_ref, *refs):
    sources_refs, out_ref, sems = refs[:-2], refs[-2], refs[-1]
    quad, member = place_ref[0], place_ref[1]
    copies = []
    for i, (ref, start, k, j) in enumerate(sources):
        q, m = lax.rem(quad + (QUADS - k), QUADS), lax.rem(member + (members - j), members)
        block = sources_refs[ref].at[pl.ds(start, rows)]
        copies.append(pltpu.make_async_copy(block, out_ref.at[q, m], sems.at[i]))
    for copy in copies:
        copy.start()
    for copy in copies:
        copy.wait()


def finish_kernel(members, sources, groups, scales, copies, place_ref, *refs):
    count = len({array for array, _, _ in groups})
    n_blocks = len({ref for ref, _, _, _ in sources})
    block_refs, refs = refs[:n_blocks], refs[n_blocks:]
    base_refs, refs = refs[:count], refs[count:]
    out_refs, refs = refs[:count], refs[count:]
    if copies:
        low_refs, refs = refs[:count], refs[count:]
        block_buf, base_buf, low_buf, sems = refs
    else:
        block_buf, base_buf, sems = refs
    quad, member = place_ref[0], place_ref[1]
    rows = block_buf.shape[2]
    loads = []
    for i, (ref, start, k, j) in enumerate(sources):
        q, m = lax.rem(quad + (QUADS - k), QUADS), lax.rem(member + (members - j), members)
        block = block_refs[ref].at[pl.ds(start, rows)]
        loads.append(pltpu.make_async_copy(block, block_buf.at[q, m], sems.at[0, i]))

    def whole_of(ref, q):
        array, at, _ = groups[q]
        return ref[array] if at is None else ref[array].at[at]

    def used(buf, q):
        return buf.at[q, pl.ds(0, members * groups[q][2])]

    bases = [pltpu.make_async_copy(whole_of(base_refs, q), used(base_buf, q), sems.at[1, q]) for q in range(QUADS)]
    for copy in loads + bases:
        copy.start()
    for copy in loads:
        copy.wait()
    stores = []
    for q in range(QUADS):
        bases[q].wait()
        own = groups[q][2]
        for m in range(members):
            at = slice(m * own, (m + 1) * own)
            value = scales[0] * base_buf[q, at] + scales[1][q] * block_buf[q, m, :own].astype(F32)
            base_buf[q, at] = value
            if copies:
                low_buf[q, at] = value.astype(BF16)
        store = [pltpu.make_async_copy(used(base_buf, q), whole_of(out_refs, q), sems.at[2, q])]
        if copies:
            store.append(pltpu.make_async_copy(used(low_buf, q), whole_of(low_refs, q), sems.at[3, q]))
        for copy in store:
            copy.start()
        stores += store
    for copy in stores:
        copy.wait()


class Blocks:
    def __init__(self, places, rows):
        self.places, self.rows = places, rows
        self.arrays, self.sources = [], []

    def add(self, array, *blocks):
        whole_tiles = all(n % 16 == 0 for n in (self.rows, *(start for start, _, _ in blocks)))
        for start, k, j in blocks:
            self.sources.append((len(self.arrays), start if whole_tiles else 0, k, j))
            if not whole_tiles:
                self.arrays.append(array[start : start + self.rows])
        if whole_tiles:
            self.arrays.append(array)

    def finished(self, arrays, groups, scales, copies=False, late=()):
        places = self.places
        away = pl.BlockSpec(memory_space=pl.ANY)
        outs = [jax.ShapeDtypeStruct(array.shape, F32) for array in arrays]
        lows = [jax.ShapeDtypeStruct(array.shape, BF16) for array in arrays] if copies else []
        if any(own % 16 for _, _, own in groups):
            blocks = self.placed(late)
            parts = [blocks[q, :, :own].reshape(-1, D).astype(F32) * scales[1][q] for q, (_, _, own) in enumerate(groups)]
            results = []
            for i, array in enumerate(arrays):
                mine = [part for part, (at, _, _) in zip(parts, groups) if at == i]
                results.append(scales[0] * array + jnp.stack(mine).reshape(array.shape))
            return results + [result.astype(BF16) for result in results if copies]
        tall = (QUADS, places.members * self.rows, D)
        return pl.pallas_call(
            lambda *refs: finish_kernel(places.members, self.sources, groups, scales, copies, *refs),
            in_specs=[pl.BlockSpec(memory_space=pltpu.SMEM)] + [away] * (len(self.arrays) + len(arrays)),
            out_specs=[away] * (len(outs) + len(lows)),
            out_shape=outs + lows,
            scratch_shapes=[
                pltpu.VMEM((QUADS, places.members, self.rows, D), BF16),
                pltpu.VMEM(tall, F32),
            ]
            + ([pltpu.VMEM(tall, BF16)] if copies else [])
            + [pltpu.SemaphoreType.DMA((4, len(self.sources)))],
            compiler_params=params(),
            name="finish",
        )(jnp.stack([places.quad, places.member]).astype(jnp.int32), *tied(self.arrays, late), *arrays)

    def placed(self, late=()):
        places = self.places
        away = pl.BlockSpec(memory_space=pl.ANY)
        return pl.pallas_call(
            lambda *refs: place_kernel(places.members, self.rows, self.sources, *refs),
            in_specs=[pl.BlockSpec(memory_space=pltpu.SMEM)] + [away] * len(self.arrays),
            out_specs=pl.BlockSpec(memory_space=pltpu.VMEM),
            out_shape=jax.ShapeDtypeStruct((QUADS, places.members, self.rows, D), BF16),
            scratch_shapes=[pltpu.SemaphoreType.DMA((len(self.sources),))],
            compiler_params=params(),
            name="place",
        )(jnp.stack([places.quad, places.member]).astype(jnp.int32), *tied(self.arrays, late))


def own_rows(places, sources, most):
    result = None
    zero = jnp.uint32(0)
    for i, (source, at) in enumerate(sources):
        rows = source.shape[1] // places.members
        part = lax.dynamic_slice(source, (jnp.uint32(at), places.member * rows, zero), (1, rows, D))[0]
        part = padded(part, most)
        result = part if result is None else jnp.where(places.quad == i, part, result)
    return result


def shards(tokens, cotangent, log_decay, w_mix, w_out, w_in, w_down, m_mix, m_out, m_in, m_down):
    places = Places()
    seqs, length, _ = tokens.shape
    count = seqs * length
    state_shape = (seqs, PAIRS, HEAD_DIM, LANES)
    tiles = D // TILE

    cot = cotangent.reshape(count, D)

    def gathered(*rows):
        return lax.all_gather(jnp.stack(rows).astype(BF16), "batch", axis=1, tiled=True)

    full_kv = gathered(w_mix[1], w_mix[2])
    full_qg = gathered(w_mix[0], w_mix[3])
    full_out = gathered(w_out)[0]
    square = jax.ShapeDtypeStruct((HEAD_COUNT, length, length), F32)
    by_lane = jax.ShapeDtypeStruct((length, D), F32)
    last, _, lead, trail, mask, mask_t = pl.pallas_call(
        decay_kernel,
        out_shape=[
            jax.ShapeDtypeStruct((HEAD_COUNT, 1), F32),
            jax.ShapeDtypeStruct((HEAD_COUNT, length), F32),
            by_lane,
            by_lane,
            square,
            square,
        ],
        compiler_params=params(),
        name="decay",
    )(log_decay)
    decays = places.gather(places.gather(last[:, 0], "members"), "quads").reshape(-1, HEAD_COUNT)
    members = places.members
    factors = pl.pallas_call(
        lambda *refs: factor_kernel(members, *refs),
        in_specs=[pl.BlockSpec(memory_space=pltpu.SMEM), pl.BlockSpec(memory_space=pltpu.VMEM)],
        out_shape=jax.ShapeDtypeStruct((2 * (2 * members + QUADS - 1), D), F32),
        compiler_params=params(),
        name="factors",
    )(jnp.stack([places.quad, places.member]).astype(jnp.int32), decays).reshape(2, -1, D)

    x = tokens.reshape(count, D)

    tile_state = pl.BlockSpec((seqs, PAIRS_PER_TILE, HEAD_DIM, LANES), lambda i: (0, i, 0, 0))
    row_state = pl.BlockSpec((1, PAIRS, HEAD_DIM, LANES), lambda i: (i, 0, 0, 0))
    tile_mask = pl.BlockSpec((HEADS_PER_TILE, length, length), lambda i: (i, 0, 0))
    pair_cols = pl.BlockSpec((2, D, TILE), lambda i: (0, 0, i))
    wide = jax.ShapeDtypeStruct((count, D), F32)
    narrow = jax.ShapeDtypeStruct((count, D), BF16)

    normed, pre_k, keys, values, summary = pl.pallas_call(
        lambda *refs: kv_kernel(seqs, *refs),
        grid=(tiles,),
        in_specs=[whole((count, D)), pair_cols, cols(length)],
        out_specs=[whole((count, D)), cols(count), cols(count), cols(count), tile_state],
        out_shape=[narrow, narrow, narrow, narrow, jax.ShapeDtypeStruct(state_shape, BF16)],
        compiler_params=params(),
        cost_estimate=cost(4 * count * D * D, 16 * count * D),
        name="kv",
    )(x, full_kv, trail)
    ahead = Carried(places, summary, factors[0], False)
    incoming = ahead.finish()

    cot_mate = places.send(tied(cot, full_kv), "core", 1)
    wide_sum = WideSum(places, w_down.shape[0])
    w_in_late, w_down_late = tied((w_in, w_down), full_kv)
    in_low, down_low = wide_sum.ordered(w_in_late), wide_sum.ordered(w_down_late[None])[0]

    pre_q, queries, gate_in, inner = pl.pallas_call(
        lambda *refs: q_kernel(seqs, *refs),
        grid=(tiles,),
        in_specs=[whole((count, D)), pair_cols, cols(count), cols(count), tile_mask],
        out_specs=[cols(count)] * 4,
        out_shape=[narrow, narrow, narrow, wide],
        compiler_params=params(),
        cost_estimate=cost(8 * count * D * D, 16 * count * D),
        name="query",
    )(normed, full_qg, keys, values, mask)

    attended, hidden, middle, normed_ffn = pl.pallas_call(
        mid_kernel,
        grid=(seqs,),
        in_specs=[
            rows_of(length),
            rows_of(length),
            row_state,
            whole((length, D)),
            rows_of(length),
            rows_of(length),
            whole((D, D)),
        ],
        out_specs=[rows_of(length)] * 4,
        out_shape=[wide, narrow, wide, narrow],
        compiler_params=params(),
        cost_estimate=cost(2 * count * D * D, 24 * count * D),
        name="middle",
    )(inner, queries, incoming, lead, gate_in, x, full_out)

    nf_mate = places.send(normed_ffn, "core", 1)
    near_weights = (in_low, down_low)
    sums, near_own = ffn(normed_ffn, cot, near_weights, (middle,))
    nf_mate, cot_mate = tied((nf_mate, cot_mate), sums)
    cut = wide_sum.cut()
    mate_sums, near = ffn(nf_mate, cot_mate, near_weights, grads=near_own[0], cut=cut)
    far_down = places.far_rows(down_low[None], full_qg, normed_ffn, mate_sums)
    far_in = places.far_rows(in_low, queries, sums, mate_sums)
    far_weights = [(part, [half[0] for half in down]) for part, down in zip(far_in, far_down)]
    place = (places.quad % 2).astype(jnp.int32).reshape(1)
    near, near_offers = wide_sum.parts(near)
    near_arrived = wide_sum.exchange(near_offers)
    far = []
    for k, weights in enumerate(far_weights):
        mate_sums = tied(mate_sums, near_offers)
        mate_sums, grad = ffn(nf_mate, cot_mate, weights, mate_sums, k == len(far_weights) - 1, place=place)
        far += grad
    out_mate, dn_mate = mate_sums
    dn_mate = places.send(dn_mate, "core", 1)
    for k, weights in enumerate(far_weights):
        sums, far[k] = ffn(normed_ffn, cot, weights, tied(sums, mate_sums), grads=far[k], cut=cut, place=place)
    far = [wide_sum.parts(grads) for grads in far]
    far_arrived = [wide_sum.exchange(offers) for _, offers in far]

    d_middle, d_attended, d_gate, local_grad = pl.pallas_call(
        gate_back_kernel,
        grid=(seqs,),
        in_specs=[
            rows_of(length),
            rows_of(length),
            rows_of(length),
            rows_of(length),
            whole((D, D)),
            rows_of(length),
            rows_of(length),
            rows_of(length),
            whole((length, D)),
        ],
        out_specs=[rows_of(length), rows_of(length), rows_of(length), row_state],
        out_shape=[narrow, narrow, narrow, jax.ShapeDtypeStruct(state_shape, BF16)],
        compiler_params=params(),
        cost_estimate=cost(2 * count * D * D, 16 * count * D),
        name="gate_back",
    )(sums[1], dn_mate, middle, cot, full_out, attended, gate_in, queries, lead)
    behind = Carried(places, local_grad, factors[1], True)
    one_cols = pl.BlockSpec((1, D, TILE), lambda i: (0, 0, i))
    four_grads = jax.ShapeDtypeStruct((4, D, D), BF16)
    out_grad, mix_grads = pl.pallas_call(
        early_grads_kernel,
        grid=(tiles,),
        in_specs=[whole((count, D)), whole((count, D)), cols(count), cols(count)],
        out_specs=[one_cols, pl.BlockSpec((1, D, TILE), lambda i: (3, 0, i))],
        out_shape=[jax.ShapeDtypeStruct((1, D, D), BF16), four_grads],
        compiler_params=params(),
        cost_estimate=cost(4 * count * D * D, 12 * count * D),
        name="early_grads",
    )(hidden, normed, d_middle, d_gate)
    d_attended = tied(d_attended, near_arrived)
    d_query, d_key_part, d_value_part, mix_grads = pl.pallas_call(
        lambda *refs: att_back_kernel(seqs, *refs),
        grid=(tiles,),
        in_specs=[cols(count)] * 5
        + [tile_mask, tile_mask, tile_state, cols(length), whole((count, D)), pl.BlockSpec(memory_space=pl.ANY)],
        out_specs=[cols(count)] * 3 + [pl.BlockSpec((1, D, TILE), lambda i: (2, 0, i))],
        out_shape=[narrow, wide, wide, four_grads],
        input_output_aliases={10: 3},
        compiler_params=params(),
        cost_estimate=cost(8 * count * D * D, 20 * count * D),
        name="attention_back",
    )(queries, keys, values, d_attended, pre_q, mask, mask_t, incoming, lead, normed, mix_grads)

    def scattered(grads):
        return lax.psum_scatter(grads, "batch", scatter_dimension=1, tiled=True)

    def members_sum(grads):
        n, rows, _ = grads.shape
        return places.scatter(grads.reshape(n, places.members, rows // places.members, D), "members", 1)

    sum_out = scattered(out_grad)
    far_sums = [
        tied(summed(own, *arrived).astype(BF16), d_query) for (own, _), arrived in zip(far, far_arrived)
    ]
    chip_arrived = [places.send(part, "chips", -(k + 1)) for k, part in enumerate(far_sums)]
    outgoing = behind.finish((d_query, far_sums, sum_out))
    out_mate = places.send(tied(out_mate, d_query), "core", 1)
    sum_out = members_sum(tied(sum_out, behind.sent))[0]
    outgoing = tied(outgoing, sum_out)
    d_normed_part = pl.pallas_call(
        dots_back_kernel,
        grid=(seqs,),
        in_specs=[rows_of(length), rows_of(length), whole((2, D, D))],
        out_specs=rows_of(length),
        out_shape=wide,
        compiler_params=params(),
        cost_estimate=cost(4 * count * D * D, 10 * count * D),
        name="normed_back",
    )(*tied((d_query, d_gate), behind.sent), full_qg)
    outgoing = tied(outgoing, d_normed_part)

    d_kv, mix_grads = pl.pallas_call(
        lambda *refs: state_back_kernel(seqs, *refs),
        grid=(tiles,),
        in_specs=[cols(count)] * 5
        + [tile_state, cols(length), whole((count, D)), pl.BlockSpec(memory_space=pl.ANY)],
        out_specs=[pl.BlockSpec((2, count, TILE), lambda i: (0, 0, i)), pair_cols],
        out_shape=[jax.ShapeDtypeStruct((2, count, D), BF16), four_grads],
        input_output_aliases={8: 1},
        compiler_params=params(),
        cost_estimate=cost(5 * count * D * D, 18 * count * D),
        name="state_back",
    )(keys, values, pre_k, d_key_part, d_value_part, outgoing, trail, normed, mix_grads)
    wide_total = summed(near, *near_arrived, *chip_arrived).astype(BF16)
    sum_out = padded(sum_out, w_down.shape[0] // places.members)
    wide_blocks = jnp.stack([wide_total[2], wide_total[0], wide_total[1], sum_out])
    wide_parts = places.scattered(wide_blocks, "quads")
    mix_sums = scattered(tied(mix_grads, chip_arrived))
    activations = (tied(sums[0], wide_blocks) + out_mate.astype(F32)).astype(BF16)
    d_kv = tied(d_kv, wide_blocks)

    input_grad = pl.pallas_call(
        input_back_kernel,
        grid=(seqs,),
        in_specs=[
            pl.BlockSpec((2, length, D), lambda i: (0, i, 0)),
            whole((2, D, D)),
            rows_of(length),
            rows_of(length),
            rows_of(length),
        ],
        out_specs=rows_of(length),
        out_shape=narrow,
        compiler_params=params(),
        cost_estimate=cost(4 * count * D * D, 16 * count * D),
        name="input_back",
    )(d_kv, full_kv, d_normed_part, x, d_middle).reshape(tokens.shape)

    wide_mom = ((m_down[None], 0), (m_in, 0), (m_in, 1), (m_out[None], 0))
    mix_mom = [(m_mix, i) for i in range(4)]

    def momentum_rows(sources, grad, after):
        arrays = tied([array for array, _ in sources], after)
        own = own_rows(places, [(array, at) for array, (_, at) in zip(arrays, sources)], grad.shape[0])
        return (MOMENTUM * own + grad.astype(F32)).astype(BF16)

    def to_members(part):
        return [places.send(part, "members", j) for j in range(1, places.members)]

    mix_split = tied(mix_sums, (input_grad, wide_parts)).reshape(4, places.members, -1, D)
    mix_offers = [
        lax.dynamic_index_in_dim(mix_split, (places.member + j) % places.members, 1, False)
        for j in range(places.members)
    ]
    mix_arrived = [places.send(part, "members", j) for j, part in enumerate(mix_offers[1:], 1)]
    wide_grad = summed(*tied(wide_parts, (activations, mix_offers))).astype(BF16)

    wide_low = momentum_rows(wide_mom, wide_grad, wide_blocks)
    wide_known = [wide_low] + to_members(wide_low)
    wide_far = [places.send(wide_low, "chips", k) for k in range(1, places.chips)]
    wide_first = places.send(tied(wide_grad, wide_low), "quads", 1)
    mix_sums = summed(*tied([mix_offers[0]] + mix_arrived, wide_low)).astype(BF16)
    mix_blocks = tied(jnp.stack([mix_sums[i] for i in (2, 0, 1, 3)]), wide_far)
    mix_parts = places.scattered(mix_blocks, "quads")
    mix_grad = summed(*mix_parts).astype(BF16)
    wide_last = [other for part in wide_far for other in to_members(part)]
    wide_known, wide_far = tied((wide_known, wide_far), (mix_parts, wide_last))
    wide_core = jnp.concatenate(wide_known + wide_far, axis=0)
    wide_every = [wide_core, places.send(wide_core, "core", 1)] + wide_last
    wide_every += [places.send(part, "core", 1) for part in wide_last]

    mix_low = momentum_rows(mix_mom, mix_grad, wide_blocks)
    rows, own = wide_grad.shape[0], mix_grad.shape[0]
    mix_others = to_members(jnp.concatenate([mix_low, mix_grad], axis=0))
    mix_known = jnp.concatenate([mix_low] + [part[:own] for part in mix_others], axis=0)
    mix_every = lax.all_gather(mix_known, "batch", axis=0, tiled=True)

    wide_all, mix_all = Blocks(places, rows), Blocks(places, own)
    wide_all.add(wide_grad, (0, 0, 0))
    wide_all.add(wide_first, (0, 1, 0))
    mix_all.add(mix_grad, (0, 0, 0))
    for j, part in enumerate(mix_others, 1):
        mix_all.add(part, (own, 0, j))
    both = jnp.concatenate([wide_grad, mix_grad], axis=0)
    mix_first = places.send(tied(mix_grad, mix_low), "quads", 1)
    second = places.send(tied(both, (mix_low, mix_first)), "quads", 2)
    early = jnp.concatenate(tied([wide_grad, wide_first], mix_known), axis=0)
    early_arrived = to_members(early)
    for j, part in enumerate(early_arrived, 1):
        wide_all.add(part, (0, 0, j), (rows, 1, j))

    wide_rows, wide_rest = newton_rows(tied(wide_every, (early, mix_known)), wide_core[: rows * places.members], rows)
    wide_x, mix_x = Blocks(places, rows), Blocks(places, own)
    wide_x.add(wide_rows, (0, 0, 0))
    wide_x.add(wide_rest, *[((j - 1) * rows, 0, j) for j in range(1, places.members)])
    second, mix_first = tied((second, mix_first), wide_rows)
    nearer = jnp.concatenate([second, mix_first], axis=0)
    nearer_arrived = to_members(nearer)
    wide_all.add(second, (0, 2, 0))
    mix_all.add(second, (rows, 2, 0))
    mix_all.add(mix_first, (0, 1, 0))
    for j, part in enumerate(nearer_arrived, 1):
        wide_all.add(part, (0, 2, j))
        mix_all.add(part, (rows, 2, j), (rows + own, 1, j))
    x_sent = tied(wide_rows, mix_every)
    x_parts = [places.send(x_sent, "quads", k) for k in (1, 2)]
    mix_rows, mix_rest = newton_rows([tied(mix_every, (wide_rows, early_arrived, nearer))], mix_known, own)
    x_pair = jnp.concatenate(tied(x_parts, (mix_rows, nearer_arrived)), axis=0)
    x_parts.append(places.send(tied(x_sent, x_pair), "quads", 3))
    third = places.send(tied(both, x_parts[2]), "quads", 3)
    for k, part in enumerate(x_parts, 1):
        wide_x.add(part, (0, k, 0))
    x_arrived = to_members(x_pair)
    for j, part in enumerate(x_arrived, 1):
        wide_x.add(part, (0, 1, j), (rows, 2, j))
    wide_all.add(third, (0, 3, 0))
    mix_all.add(third, (rows, 3, 0))
    for j, part in enumerate(to_members(third), 1):
        wide_all.add(part, (0, 3, j))
        mix_all.add(part, (rows, 3, j))
    mix_x.add(mix_rows, (0, 0, 0))
    mix_x.add(mix_rest, *[((j - 1) * own, 0, j) for j in range(1, places.members)])
    mix_sent = tied(mix_rows, x_arrived)
    mix_parts = [places.send(mix_sent, "quads", k) for k in (1, 2, 3)]
    x_last = to_members(x_parts[2])
    for j, part in enumerate(x_last, 1):
        wide_x.add(part, (0, 3, j))
    for k, part in enumerate(mix_parts, 1):
        mix_x.add(part, (0, k, 0))
    for j, part in enumerate(to_members(jnp.concatenate(tied(mix_parts, x_last), axis=0)), 1):
        mix_x.add(part, *[((k - 1) * own, k, j) for k in (1, 2, 3)])

    hidden_rows, width_rows = w_down.shape[0] // places.members, w_out.shape[0] // places.members
    wide_groups = [(0, None, hidden_rows), (1, 0, hidden_rows), (1, 1, hidden_rows), (2, None, width_rows)]
    mix_groups = [(0, i, width_rows) for i in range(4)]
    ones = [1.0] * 4
    factor = math.sqrt(FF / D)
    steps = [-STEP_RATE, -STEP_RATE * factor, -STEP_RATE * factor, -STEP_RATE]
    new_down, new_in, new_out, copy_down, copy_in, copy_out = wide_x.finished(
        (w_down, w_in, w_out), wide_groups, (1.0, steps), True
    )
    mom_down, mom_in, mom_out = wide_all.finished(
        (m_down, m_in, m_out), wide_groups, (MOMENTUM, ones), late=new_in
    )
    (mom_mix,) = mix_all.finished((m_mix,), mix_groups, (MOMENTUM, ones), late=mom_in)
    new_mix, copy_mix = mix_x.finished((w_mix,), mix_groups, (1.0, [-STEP_RATE] * 4), True, late=mom_mix)
    return (
        activations.reshape(tokens.shape),
        input_grad,
        mom_mix,
        mom_out,
        mom_in,
        mom_down,
        new_mix,
        new_out,
        new_in,
        new_down,
        copy_mix,
        copy_out,
        copy_in,
        copy_down,
    )


def solution(mesh):
    batch_rows = P(None, "batch", None)
    flat_rows = P("batch", None)
    block = P("batch", "seq", None)
    four = (batch_rows, flat_rows, batch_rows, flat_rows)
    in_specs = (block, block, P(None, "seq")) + four + four
    out_specs = (block, block) + four + four + four
    return jax.shard_map(shards, mesh=mesh, in_specs=in_specs, out_specs=out_specs, check_vma=False)
```
